256 devices in a mesh: group: 4 (over x_hi, core), shard: 64 (over y, z, x_lo).
Axes of the slice: x: 4 (x_hi: 2, x_lo: 2; x = x_hi * 2 + x_lo), y: 4, z: 8, core: 2. Of those that a mesh axis runs over, the one named last changes fastest.
Arguments:
- queries: bfloat16 [16, 16, 5120], P('group'), may hold values from -150 to 150
- fresh_kv: bfloat16 [2, 16, 16, 1024], P(None, 'group'), may hold values from -4.5 to 4.5
- kv_pages: bfloat16 [2, 256, 128, 1024], P(None, ('group', 'shard')), may hold values from -4.5 to 4.5
- page_list: int32 [16, 64], P('group'), may hold values from 0 to 255, as said below
- tile_mask: int32 [16, 64], P('group'), may hold values from 0 to 1, as said below
- out_weight: bfloat16 [5120, 5120], P('shard'), may hold values from -0.078125 to 0.078125
Outputs:
- block_output: bfloat16 [16, 16, 5120], P('group', None, 'shard')
The draws below stay inside these ranges and needn't reach their ends.
Inputs may be any that keep to these rules, and one draw needn't show every extreme that they name: `page_list`: each branch's 64 page numbers are different. `tile_mask`: the valid slots of a branch are the first 16 to 64 of its list; some branch has all 64 valid.
All inputs are finite; a program needn't handle non-finite values.
Results may differ from the reference program's by a relative error of at most 0.03.
Values may be sent and summed in bfloat16 or wider, within the bound.
A program may use at most 192 MiB of HBM per device.

```python
import math
import jax
import jax.numpy as jnp
from jax import lax

D = 5120
Q_HEADS = 40
KV_HEADS = 8
HEAD_DIM = 128
PAGE = 128
BLOCK_TOK = 16
PAGES = 256
LIST = 64
BRANCHES = 16


def drawn_draw(key):
    fresh_pair = jnp.clip(jax.random.normal(jax.random.fold_in(key, 101), (2, BRANCHES, BLOCK_TOK, KV_HEADS * HEAD_DIM), jnp.float32), -4.5, 4.5)
    query_draw = jnp.clip(jax.random.normal(jax.random.fold_in(key, 102), (BRANCHES, BLOCK_TOK, Q_HEADS * HEAD_DIM), jnp.float32), -4.5, 4.5)
    key_heads = fresh_pair[0].reshape(BRANCHES, BLOCK_TOK, KV_HEADS, HEAD_DIM)
    query_heads = query_draw.reshape(BRANCHES, BLOCK_TOK, Q_HEADS, HEAD_DIM)
    new_keys = key_heads.reshape(BRANCHES, BLOCK_TOK, KV_HEADS * HEAD_DIM)
    fresh_pair = jnp.stack([new_keys, fresh_pair[1]])
    return (query_heads.reshape(BRANCHES, BLOCK_TOK, Q_HEADS * HEAD_DIM), fresh_pair)


def draw_queries(key, part):
    drawn = drawn_draw(key)
    return drawn[0].astype(jnp.bfloat16)


def draw_fresh_kv(key, part):
    drawn = drawn_draw(key)
    return drawn[1].astype(jnp.bfloat16)


def draw_page_list(key, part):
    key = jax.random.fold_in(key, 7)
    branch_keys = jax.random.split(key, BRANCHES)
    picked = jax.vmap(lambda single: jax.random.permutation(single, PAGES)[:LIST])(branch_keys)
    return picked.astype(jnp.int32)


def draw_tile_mask(key, part):
    key = jax.random.fold_in(key, 8)
    lengths = jax.random.randint(jax.random.fold_in(key, 1), (BRANCHES,), LIST // 4, LIST + 1)
    fullest = jax.random.randint(jax.random.fold_in(key, 2), (), 0, BRANCHES)
    lengths = jnp.where(jnp.arange(BRANCHES) == fullest, LIST, lengths)
    return (jnp.arange(LIST)[None, :] < lengths[:, None]).astype(jnp.int32)


def steps_of(own_key, extent, pieces, smallest, top_value):
    level = 1.0
    for axis_at, parts in pieces:
        heights = jax.random.uniform(jax.random.fold_in(jax.random.fold_in(own_key, 6), axis_at), (parts,), jnp.float32, smallest / len(pieces), top_value / len(pieces))
        level = level * jnp.repeat(jnp.exp(heights), extent[axis_at] // parts).reshape((-1,) + (1,) * (len(extent) - 1 - axis_at))
    return level


def scatter_about(key, shape, width, bound, pieces=(), kind=jnp.bfloat16):
    values = width * jax.random.normal(key, shape, jnp.float32)
    if pieces:
        values = values * steps_of(key, shape, pieces, -0.22, 0.18)
    return jnp.clip(values, -bound, bound).astype(kind)


def setup_inputs(seed: int = 0) -> dict:
    arg_keys = jax.random.split(jax.random.key(seed), 7)
    queries = draw_queries(jax.random.fold_in(arg_keys[6], 71), 0)
    fresh_kv = draw_fresh_kv(jax.random.fold_in(arg_keys[6], 71), 0)
    kv_pages = scatter_about(arg_keys[2], (2, PAGES, PAGE, KV_HEADS * HEAD_DIM), 1.0, 4.5, ((1, 256),))
    page_list = draw_page_list(jax.random.fold_in(arg_keys[6], 71), 0)
    tile_mask = draw_tile_mask(jax.random.fold_in(arg_keys[6], 71), 0)
    out_weight = scatter_about(arg_keys[5], (Q_HEADS * HEAD_DIM, D), (Q_HEADS * HEAD_DIM) ** -0.5, 0.078125, ((0, 64),))
    return dict(queries=queries, fresh_kv=fresh_kv, kv_pages=kv_pages, page_list=page_list, tile_mask=tile_mask, out_weight=out_weight)


def reference(queries, fresh_kv, kv_pages, page_list, tile_mask, out_weight):
    kv_width = KV_HEADS * HEAD_DIM
    group_size = Q_HEADS // KV_HEADS
    scaling = 1.0 / math.sqrt(HEAD_DIM)
    causal = jnp.arange(BLOCK_TOK)[None, :] <= jnp.arange(BLOCK_TOK)[:, None]
    listed = LIST * PAGE

    def one_branch(items):
        query_rows, own_tokens, page_ids, page_valid = items
        key_rows = jnp.concatenate([kv_pages[0][page_ids].reshape(listed, kv_width), own_tokens[0]], 0)
        value_rows = jnp.concatenate([kv_pages[1][page_ids].reshape(listed, kv_width), own_tokens[1]], 0)
        page_ok = jnp.repeat(page_valid > 0, PAGE)
        visible = jnp.concatenate([jnp.broadcast_to(page_ok[None, :], (BLOCK_TOK, listed)), causal], 1)
        query_heads = query_rows.astype(jnp.float32).reshape(BLOCK_TOK, KV_HEADS, group_size, HEAD_DIM)
        key_heads = key_rows.astype(jnp.float32).reshape(-1, KV_HEADS, HEAD_DIM)
        value_heads = value_rows.astype(jnp.float32).reshape(-1, KV_HEADS, HEAD_DIM)
        scores = jnp.einsum('thgd,nhd->hgtn', query_heads, key_heads) * scaling
        masked = jnp.where(visible[None, None], scores, -1e+30)
        highest = lax.optimization_barrier(jnp.max(masked, axis=-1, keepdims=True))
        weights = jnp.where(visible[None, None], jnp.exp(masked - highest), 0.0)
        totals = lax.optimization_barrier(jnp.sum(weights, axis=-1))
        rounded = lax.optimization_barrier(weights.astype(jnp.bfloat16)).astype(jnp.float32)
        summed = jnp.einsum('hgtn,nhd->thgd', rounded, value_heads)
        normed = summed / jnp.moveaxis(totals, 2, 0)[..., None]
        return normed.reshape(BLOCK_TOK, Q_HEADS * HEAD_DIM).astype(jnp.bfloat16)
    attention = lax.map(one_branch, (queries, jnp.moveaxis(fresh_kv, 1, 0), page_list, tile_mask))
    flattened = attention.reshape(BRANCHES * BLOCK_TOK, Q_HEADS * HEAD_DIM)
    projected = jnp.dot(flattened, out_weight, preferred_element_type=jnp.float32)
    return projected.astype(jnp.bfloat16).reshape(BRANCHES, BLOCK_TOK, D)
```

```python
import functools
import math

import jax
import jax.numpy as jnp
from jax import lax
from jax.experimental import pallas as pl
from jax.experimental.pallas import tpu as pltpu
from jax.sharding import PartitionSpec as P

MESH = pl.DeviceIdType.MESH
BF, F32 = jnp.bfloat16, jnp.float32
HIDDEN = -1e30
FLOOR = -1e29


def device(h, m, y, z, c):
    return (h * 2 + c, (y * 8 + z) * 2 + (m + h) % 2)


def kernel(
    q_hbm, f_hbm, kv_hbm, list_ref, mask_ref, w_hbm, out_ref,
    qb, qc, kvb, fb, eb, bias, m_ref, l_ref, acc, wv, wp, wb,
    accs, sts, accr, strv, attp, att_t, os, orv,
    loc, pg_s, pg_r, fw_s, fw_r, q_s, q_r, w_s, w_r, wf_s, wf_r,
    ac_s, ac_r, st_s, st_r, at_s, at_r, o_s, o_r,
):
    g = lax.axis_index("group")
    s = lax.axis_index("shard")
    h, c = g // 2, g % 2
    y, z, l = s // 16, (s // 2) % 8, s % 2
    m = (l + h) % 2
    head = 2 * y + m
    plane = [(dm, dy) for dm in range(2) for dy in range(4)]
    column = [(dh, dz) for dh in range(2) for dz in range(8)]
    sibling = device(h, m, y, z, 1 - c)
    across = device(1 - h, m, y, z, c)

    def in_plane(j):
        dm, dy = plane[j]
        return device(h, (m + dm) % 2, (y + dy) % 4, z, c)

    def in_column(k):
        dh, dz = column[k]
        return device((h + dh) % 2, m, y, (z + dz) % 8, c)

    def w_to(k):
        return z // 4, 2 * k + (z + c) % 2

    def w_from(k):
        return (k % 2 + h) % 2, 4 * m + 2 * (k // 2) + (z + c) % 2

    def w_slot(zz, ll):
        return (zz % 4) * 2 + ll

    bar = pltpu.get_barrier_semaphore()

    def greet(d):
        pl.semaphore_signal(bar, inc=1, device_id=d, device_id_type=MESH)

    greet(sibling)
    for j in range(1, 8):
        greet(in_plane(j))
    for k in range(1, 16):
        greet(in_column(k))
    for k in range(4):
        m2, z2 = w_from(k)
        pl.when((m2 != m) | (z2 != z))(functools.partial(greet, device(h, m2, y, z2, c)))
    w_self = (z // 4 == m) & (c == 0)

    cols = pl.ds(pl.multiple_of(head * 128, 128), 128)
    q_cols = pl.ds(pl.multiple_of(head * 640, 128), 640)
    ld_q = pltpu.make_async_copy(q_hbm.at[:, q_cols], qb.at[0], loc.at[0])
    ld_kv = pltpu.make_async_copy(kv_hbm.at[:, :, cols], kvb.at[:, 0], loc.at[1])
    ld_f = pltpu.make_async_copy(f_hbm.at[:, :, cols], fb, loc.at[2])
    ld_w = pltpu.make_async_copy(w_hbm, wv, loc.at[3])
    ld_w.start()
    ld_q.start()
    ld_kv.start()
    ld_f.start()

    eb[0] = jnp.full((8, 128), -1, jnp.int32)
    eb[0, 0:4, 0:64] = jnp.where(mask_ref[...] > 0, list_ref[...], -1)

    ld_w.wait()
    for z2 in range(8):
        wp[z2] = jnp.concatenate(
            [wv[:, 1280 * y2 + 160 * z2 : 1280 * y2 + 160 * z2 + 160] for y2 in range(4)], axis=1
        )

    pl.semaphore_wait(bar, 27 - w_self.astype(jnp.int32))

    def send(src, dst, ss, rs, d):
        cp = pltpu.make_async_remote_copy(
            src_ref=src, dst_ref=dst, send_sem=ss, recv_sem=rs, device_id=d, device_id_type=MESH
        )
        cp.start()
        return cp

    sent = []
    snd_e = send(eb.at[0], eb.at[1], q_s.at[0], q_r.at[0], across)
    pages = [None] * 8
    for j in (6, 2, 7, 5, 3, 1, 4):
        dm, dy = plane[j]
        there = 2 * ((y + dy) % 4) + (m + dm) % 2
        there_cols = pl.ds(pl.multiple_of(there * 128, 128), 128)
        pages[j] = send(kv_hbm.at[:, :, there_cols], kvb.at[:, j], pg_s.at[j], pg_r.at[j], in_plane(j))
    ld_q.wait()
    snd_q = send(qb.at[0], qb.at[1], q_s.at[1], q_r.at[1], across)
    ld_kv.wait()
    forwards = [None] * 8
    forwards[0] = send(kvb.at[:, 0], kvb.at[:, 8], fw_s.at[0], fw_r.at[0], sibling)

    for k in range(4):
        m2, z2 = w_to(k)
        here = (m2 == m) & (z2 == z)
        rows = pl.ds(pl.multiple_of(80 * w_slot(z, l), 16), 80)
        slot = ((z % 4) // 2) * 2 + l

        @pl.when(here)
        def _():
            pltpu.make_async_copy(wp.at[z2], wb.at[rows], loc.at[4]).start()

        @pl.when(jnp.logical_not(here))
        def _():
            send(wp.at[z2], wb.at[rows], w_s.at[k], w_r.at[slot], device(h, m2, y, z2, c))

    snd_e.wait_recv()
    lists = eb[...].reshape(16, 128)
    row = lax.broadcasted_iota(jnp.int32, (16, 640), 0)
    col = lax.broadcasted_iota(jnp.int32, (16, 640), 1)
    owner = jnp.where(col >= 320, 8, 0) + ((col >> 4) & 3)
    pick = (row == owner).astype(F32)
    for j in range(16):
        dm, dy = plane[j % 8]
        src_m, src_y, src_c = (m - dm + 2) % 2, (y - dy + 4) % 4, (c + j // 8) % 2
        src_l = (src_m + h) % 2
        number = (h * 2 + src_c) * 64 + (src_y * 8 + z) * 2 + src_l
        seen = jnp.max((lists == number).astype(F32), axis=1, keepdims=True)
        bias[pl.ds(j, 1), :] = (jnp.sum(pick * seen, axis=0, keepdims=True) - 1.0) * (-HIDDEN)

    snd_q.wait_recv()
    for o in range(2):
        for i in range(5):
            qc[o * 320 + i * 64 : o * 320 + i * 64 + 64, :] = qb[o, :, i * 128 : i * 128 + 128]

    scale = math.log2(math.e) / math.sqrt(128)

    def scores(keys):
        return lax.dot_general(keys, qc[...], (((1,), (1,)), ((), ())), preferred_element_type=F32) * scale

    def weigh(values, weights):
        return lax.dot_general(
            values, weights.astype(BF), (((0,), (0,)), ((), ())), preferred_element_type=F32
        )

    ld_f.wait()
    key = lax.broadcasted_iota(jnp.int32, (64, 640), 0)
    col = lax.broadcasted_iota(jnp.int32, (64, 640), 1)
    visible = (col < 320) & ((key >> 4) == ((col >> 4) & 3)) & ((key & 15) <= (col & 15)) & (z == 0)
    sc = jnp.where(visible, scores(fb[0]), HIDDEN)
    top = jnp.maximum(jnp.max(sc, axis=0, keepdims=True), FLOOR)
    wt = jnp.exp2(sc - top)
    m_ref[...] = top
    l_ref[...] = jnp.sum(wt, axis=0, keepdims=True)
    acc[...] = weigh(fb[1], wt)

    def block(first):
        sc = scores(kvb[0, first : first + 4].reshape(512, 128))
        sc = (sc.reshape(4, 128, 640) + bias[first : first + 4, :][:, None, :]).reshape(512, 640)
        old = m_ref[...]
        top = jnp.maximum(old, jnp.max(sc, axis=0, keepdims=True))
        keep = jnp.exp2(old - top)
        wt = jnp.exp2(sc - top)
        m_ref[...] = top
        l_ref[...] = l_ref[...] * keep + jnp.sum(wt, axis=0, keepdims=True)
        acc[...] = acc[...] * keep + weigh(kvb[1, first : first + 4].reshape(512, 128), wt)

    def pass_on(j):
        pages[j].wait_recv()
        forwards[j] = send(kvb.at[:, j], kvb.at[:, 8 + j], fw_s.at[j], fw_r.at[j], sibling)

    for j in (1, 3, 2):
        pass_on(j)
    block(0)
    for j in (4, 5, 7, 6):
        pass_on(j)
    for j in range(4):
        forwards[j].wait_recv()
    block(8)
    block(4)
    for j in range(4, 8):
        forwards[j].wait_recv()
    block(12)

    nil = jnp.zeros((128, 64), F32)
    for o in range(2):
        at = slice(o * 320, o * 320 + 320)
        accs[o] = jnp.concatenate([acc[:, at], nil], axis=1).astype(BF)
        sts[o] = jnp.concatenate(
            [jnp.concatenate([m_ref[:, at], l_ref[:, at]], axis=0), nil[0:2]], axis=1
        )
    parts, stats = [None] * 16, [None] * 16
    for k in (12, 4, 11, 13, 3, 5, 10, 14, 2, 6, 9, 15, 1, 7, 8):
        dh, dz = column[k]
        rows = pl.ds(pl.multiple_of(16 * ((z + dz) % 8), 16), 16)
        stats[k] = send(sts.at[dh], strv.at[k], st_s.at[k], st_r.at[k], in_column(k))
        parts[k] = send(accs.at[dh, rows], accr.at[k], ac_s.at[k], ac_r.at[k], in_column(k))
    mine = pl.ds(pl.multiple_of(16 * z, 16), 16)
    accr[0] = accs[0, mine, :]
    strv[0] = sts[0]

    w_fwd = []
    for k in range(4):
        m2, z2 = w_from(k)
        here = (m2 == m) & (z2 == z)
        rows = pl.ds(pl.multiple_of(80 * w_slot(z2, k % 2), 16), 80)

        @pl.when(here)
        def _():
            pltpu.make_async_copy(wp.at[z2], wb.at[rows], loc.at[4]).wait()

        @pl.when(jnp.logical_not(here))
        def _():
            pltpu.make_async_remote_copy(
                src_ref=wp.at[0], dst_ref=wb.at[rows], send_sem=w_s.at[k], recv_sem=w_r.at[k],
                device_id=sibling, device_id_type=MESH,
            ).wait_recv()

        w_fwd.append(send(wb.at[rows], wb.at[rows], wf_s.at[k], wf_r.at[k], sibling))

    for k in range(1, 16):
        stats[k].wait_recv()
    tops, sums = strv[:, 0, :], strv[:, 1, :]
    top = jnp.max(tops, axis=0, keepdims=True)
    factor = jnp.exp2(tops - top)
    factor = factor / jnp.sum(factor * sums, axis=0, keepdims=True)
    total = jnp.zeros((16, 384), F32)
    for k in range(16):
        if k:
            parts[k].wait_recv()
        total = total + accr[k].astype(F32) * factor[k : k + 1, :]
    attp[...] = total.astype(BF)

    gathered = [None] * 8
    for dz in (4, 3, 5, 2, 6, 1, 7):
        gathered[dz] = send(attp, att_t.at[mine], at_s.at[dz], at_r.at[dz], in_column(dz))
    att_t[mine, :] = attp[...]
    for k in range(4):
        w_fwd[k].wait_recv()
    for dz in range(1, 8):
        gathered[dz].wait_recv()

    att = att_t[...].astype(F32).T.astype(BF)
    proj = jnp.zeros((64, 640), F32)
    for i in range(5):
        proj += jnp.dot(att[i * 64 : i * 64 + 64], wb[i * 128 : i * 128 + 128, :], preferred_element_type=F32)
    for k in range(8):
        os[k] = jnp.concatenate([proj[:, 80 * k : 80 * k + 80], jnp.zeros((64, 48), F32)], axis=1).astype(BF)
    outs = [None] * 8
    for j in (6, 2, 7, 5, 3, 1, 4):
        dm, dy = plane[j]
        k = 2 * ((y + dy) % 4) + ((m + dm) % 2 + h) % 2
        outs[j] = send(os.at[k], orv.at[j], o_s.at[j], o_r.at[j], in_plane(j))
    result = os[2 * y + l].astype(F32)
    for j in range(1, 8):
        outs[j].wait_recv()
        result += orv[j].astype(F32)
    out_ref[...] = result[:, :80].astype(BF)

    snd_e.wait_send()
    snd_q.wait_send()
    for j in range(8):
        if j:
            pages[j].wait_send()
            outs[j].wait_send()
            gathered[j].wait_send()
        forwards[j].wait_send()
    for k in range(1, 16):
        stats[k].wait_send()
        parts[k].wait_send()
    for k in range(4):
        w_fwd[k].wait_send()
        m2, z2 = w_to(k)

        @pl.when((m2 != m) | (z2 != z))
        def _():
            pltpu.make_async_remote_copy(
                src_ref=wp.at[z2], dst_ref=wb.at[pl.ds(0, 80)], send_sem=w_s.at[k], recv_sem=w_r.at[k],
                device_id=sibling, device_id_type=MESH,
            ).wait_send()


def on_device(queries, fresh_kv, kv_pages, page_list, tile_mask, out_weight):
    any_spec, vmem = pl.BlockSpec(memory_space=pl.ANY), pl.BlockSpec(memory_space=pltpu.VMEM)
    sem = lambda n: pltpu.SemaphoreType.DMA((n,))
    out = pl.pallas_call(
        kernel,
        out_shape=jax.ShapeDtypeStruct((64, 80), BF),
        in_specs=[any_spec, any_spec, any_spec, vmem, vmem, any_spec],
        out_specs=vmem,
        scratch_shapes=[
            pltpu.VMEM((2, 64, 640), BF),
            pltpu.VMEM((640, 128), BF),
            pltpu.VMEM((2, 16, 128, 128), BF),
            pltpu.VMEM((2, 64, 128), BF),
            pltpu.VMEM((2, 8, 128), jnp.int32),
            pltpu.VMEM((16, 640), F32),
            pltpu.VMEM((1, 640), F32),
            pltpu.VMEM((1, 640), F32),
            pltpu.VMEM((128, 640), F32),
            pltpu.VMEM((80, 5120), BF),
            pltpu.VMEM((8, 80, 640), BF),
            pltpu.VMEM((640, 640), BF),
            pltpu.VMEM((2, 128, 384), BF),
            pltpu.VMEM((2, 2, 384), F32),
            pltpu.VMEM((16, 16, 384), BF),
            pltpu.VMEM((16, 2, 384), F32),
            pltpu.VMEM((16, 384), BF),
            pltpu.VMEM((128, 384), BF),
            pltpu.VMEM((8, 64, 128), BF),
            pltpu.VMEM((8, 64, 128), BF),
            sem(5), sem(8), sem(8), sem(8), sem(8), sem(2), sem(2), sem(4), sem(4), sem(4), sem(4),
            sem(16), sem(16), sem(16), sem(16), sem(8), sem(8), sem(8), sem(8),
        ],
        compiler_params=pltpu.CompilerParams(
            collective_id=0, has_side_effects=True, vmem_limit_bytes=40 * 2**20
        ),
        name="attend",
    )(
        queries.reshape(64, 5120),
        fresh_kv.reshape(2, 64, 1024),
        kv_pages.reshape(2, 128, 1024),
        page_list,
        tile_mask,
        out_weight,
    )
    return out.reshape(4, 16, 80)


def solution(mesh):
    return jax.shard_map(
        on_device,
        mesh=mesh,
        in_specs=(
            P("group", None, None),
            P(None, "group", None, None),
            P(None, ("group", "shard"), None, None),
            P("group", None),
            P("group", None),
            P("shard", None),
        ),
        out_specs=P("group", None, "shard"),
        check_vma=False,
    )
```

```python
import functools
import math

import jax
import jax.numpy as jnp
from jax import lax
from jax.experimental import pallas as pl
from jax.experimental.pallas import tpu as pltpu
from jax.sharding import PartitionSpec as P

MESH = pl.DeviceIdType.MESH
BF, F32 = jnp.bfloat16, jnp.float32
HIDDEN = -1e30
FLOOR = -1e29


def device(h, m, y, z, c):
    return (h * 2 + c, (y * 8 + z) * 2 + (m + h) % 2)


def kernel(
    q_hbm, f_hbm, kv_hbm, list_hbm, mask_hbm, w_hbm, out_ref,
    list_ref, mask_ref, qb, qc, kvb, fb, eb, bias, m_ref, l_ref, acc, wv, wp, wb,
    msg, accr, attp, att_g, os, orv,
    loc, pg_s, pg_r, fw_s, fw_r, q_s, q_r, w_s, w_r, wx_s, wx_r, wf_s, wf_r,
    ac_s, ac_r, at_s, at_r, o_s, o_r,
):
    g = lax.axis_index("group")
    s = lax.axis_index("shard")
    h, c = g // 2, g % 2
    y, z, l = s // 16, (s // 2) % 8, s % 2
    m = (l + h) % 2
    head = 2 * y + m
    plane = [(0, 0), (1, 0), (0, 1), (0, 3), (1, 1), (1, 3), (0, 2), (1, 2)]
    column = [(dh, dz) for dh in range(2) for dz in range(8)]
    sibling = device(h, m, y, z, 1 - c)
    across = device(1 - h, m, y, z, c)

    def in_plane(j):
        dm, dy = plane[j]
        return device(h, (m + dm) % 2, (y + dy) % 4, z, c)

    def in_column(k):
        dh, dz = column[k]
        return device((h + dh) % 2, m, y, (z + dz) % 8, c)

    holder = z // 4 == m
    w_to = [2 * k + (z + c) % 2 for k in range(4)]
    w_from = [4 * m + 2 * k + (z + c) % 2 for k in range(2)]

    def w_rows(zz, ll):
        return pl.ds(pl.multiple_of(80 * ((zz % 4) * 2 + ll), 16), 80)

    bar = pltpu.get_barrier_semaphore()

    def greet(d):
        pl.semaphore_signal(bar, inc=1, device_id=d, device_id_type=MESH)

    greet(sibling)
    for j in range(1, 8):
        greet(in_plane(j))
    for k in range(1, 16):
        greet(in_column(k))

    cols = pl.ds(pl.multiple_of(head * 128, 128), 128)
    q_cols = pl.ds(pl.multiple_of(head * 640, 128), 640)
    ld_q = pltpu.make_async_copy(q_hbm.at[:, q_cols], qb.at[0], loc.at[0])
    ld_kv = pltpu.make_async_copy(kv_hbm.at[:, :, cols], kvb.at[:, 0], loc.at[1])
    ld_f = pltpu.make_async_copy(f_hbm.at[:, :, cols], fb, loc.at[2])
    ld_w = pltpu.make_async_copy(w_hbm, wv, loc.at[3])
    ld_list = pltpu.make_async_copy(list_hbm, list_ref, loc.at[5])
    ld_mask = pltpu.make_async_copy(mask_hbm, mask_ref, loc.at[6])
    for ld in (ld_list, ld_mask, ld_q, ld_kv, ld_w, ld_f):
        ld.start()

    eb[0] = jnp.full((8, 128), -1, jnp.int32)
    ld_list.wait()
    ld_mask.wait()
    eb[0, 0:4, 0:64] = jnp.where(mask_ref[...] > 0, list_ref[...], -1)

    ld_w.wait()
    for z2 in range(8):
        wp[z2] = jnp.concatenate(
            [wv[:, 1280 * y2 + 160 * z2 : 1280 * y2 + 160 * z2 + 160] for y2 in range(4)], axis=1
        )

    pl.semaphore_wait(bar, 23)

    def send(src, dst, ss, rs, d):
        cp = pltpu.make_async_remote_copy(
            src_ref=src, dst_ref=dst, send_sem=ss, recv_sem=rs, device_id=d, device_id_type=MESH
        )
        cp.start()
        pending.append(cp)
        return cp

    pending = []
    snd_e = send(eb.at[0], eb.at[1], q_s.at[0], q_r.at[0], across)
    pages = [None] * 8
    for j in range(1, 8):
        dm, dy = plane[j]
        there = 2 * ((y + dy) % 4) + (m + dm) % 2
        there_cols = pl.ds(pl.multiple_of(there * 128, 128), 128)
        pages[j] = send(kv_hbm.at[:, :, there_cols], kvb.at[:, j], pg_s.at[j], pg_r.at[j], in_plane(j))
    ld_q.wait()
    snd_q = send(qb.at[0], qb.at[1], q_s.at[1], q_r.at[1], across)
    ld_kv.wait()

    forwards = [None] * 8
    forwards[0] = send(kvb.at[:, 0], kvb.at[:, 8], fw_s.at[0], fw_r.at[0], sibling)

    def w_send(k, slot):
        return pltpu.make_async_remote_copy(
            src_ref=wp.at[w_to[k]], dst_ref=wb.at[w_rows(z, l)], send_sem=w_s.at[k], recv_sem=w_r.at[slot],
            device_id=device(h, m, y, w_to[k], c), device_id_type=MESH,
        )

    def w_keep():
        return pltpu.make_async_copy(wp.at[z], wb.at[w_rows(z, l)], loc.at[4])

    for k in range(4):
        pl.when(holder & (w_to[k] != z))(lambda: w_send(k, (z % 4) // 2).start())
    pl.when(holder & (c == 0))(lambda: w_keep().start())

    def pass_weights_on():
        for k in range(2):
            mine = w_from[k] == z
            pl.when(mine)(lambda: w_keep().wait())
            pl.when(jnp.logical_not(mine))(lambda: w_send(k, k).wait_recv())
            rows = wb.at[w_rows(w_from[k], l)]
            w_cross.append(send(rows, rows, wx_s.at[k], wx_r.at[k], across))
            w_fwd.append(send(rows, rows, wf_s.at[k], wf_r.at[k], sibling))

    def pass_crossed_weights_on():
        for k in range(2):
            w_cross[k].wait_recv()
            rows = wb.at[w_rows(w_from[k], 1 - l)]
            w_fwd.append(send(rows, rows, wf_s.at[2 + k], wf_r.at[2 + k], sibling))

    w_cross, w_fwd = [], []

    def finish():
        for cp in pending:
            cp.wait_send()
        for k in range(4):
            pl.when(holder & (w_to[k] != z))(lambda: w_send(k, 0).wait_send())

    snd_e.wait_recv()
    lists = eb[...].reshape(16, 128)
    row = lax.broadcasted_iota(jnp.int32, (16, 640), 0)
    col = lax.broadcasted_iota(jnp.int32, (16, 640), 1)
    owner = jnp.where(col >= 320, 8, 0) + ((col >> 4) & 3)
    pick = (row == owner).astype(F32)
    for j in range(16):
        dm, dy = plane[j % 8]
        src_m, src_y, src_c = (m - dm + 2) % 2, (y - dy + 4) % 4, (c + j // 8) % 2
        src_l = (src_m + h) % 2
        number = (h * 2 + src_c) * 64 + (src_y * 8 + z) * 2 + src_l
        seen = jnp.max((lists == number).astype(F32), axis=1, keepdims=True)
        bias[pl.ds(j, 1), :] = (jnp.sum(pick * seen, axis=0, keepdims=True) - 1.0) * (-HIDDEN)

    snd_q.wait_recv()
    for o in range(2):
        for i in range(5):
            qc[o * 320 + i * 64 : o * 320 + i * 64 + 64, :] = qb[o, :, i * 128 : i * 128 + 128]

    scale = math.log2(math.e) / math.sqrt(128)

    def scores(keys):
        return lax.dot_general(keys, qc[...], (((1,), (1,)), ((), ())), preferred_element_type=F32) * scale

    def weigh(values, weights):
        return lax.dot_general(
            values, weights.astype(BF), (((0,), (0,)), ((), ())), preferred_element_type=F32
        )

    ld_f.wait()
    key = lax.broadcasted_iota(jnp.int32, (64, 640), 0)
    col = lax.broadcasted_iota(jnp.int32, (64, 640), 1)
    visible = (col < 320) & ((key >> 4) == ((col >> 4) & 3)) & ((key & 15) <= (col & 15)) & (z == 0)
    sc = jnp.where(visible, scores(fb[0]), HIDDEN)
    top = jnp.maximum(jnp.max(sc, axis=0, keepdims=True), FLOOR)
    wt = jnp.exp2(sc - top)
    m_ref[...] = top
    l_ref[...] = jnp.sum(wt, axis=0, keepdims=True)
    acc[...] = weigh(fb[1], wt)

    def block(first):
        sc = scores(kvb[0, first : first + 4].reshape(512, 128))
        sc = (sc.reshape(4, 128, 640) + bias[first : first + 4, :][:, None, :]).reshape(512, 640)
        old = m_ref[...]
        top = jnp.maximum(old, jnp.max(sc, axis=0, keepdims=True))
        keep = jnp.exp2(old - top)
        wt = jnp.exp2(sc - top)
        m_ref[...] = top
        l_ref[...] = l_ref[...] * keep + jnp.sum(wt, axis=0, keepdims=True)
        acc[...] = acc[...] * keep + weigh(kvb[1, first : first + 4].reshape(512, 128), wt)

    def pass_on(j):
        pages[j].wait_recv()
        forwards[j] = send(kvb.at[:, j], kvb.at[:, 8 + j], fw_s.at[j], fw_r.at[j], sibling)

    for j in range(1, 4):
        pass_on(j)
    block(0)
    for j in range(4):
        forwards[j].wait_recv()
    block(8)
    for j in range(4, 8):
        pass_on(j)
    block(4)
    for j in range(4, 8):
        forwards[j].wait_recv()
    block(12)

    def pieces(x, n):
        out = []
        for _ in range(n):
            out.append(x.astype(BF).astype(F32))
            x = x - out[-1]
        return out

    sums_rows = acc[...].T
    stats = jnp.concatenate(
        pieces(m_ref[...], 3) + pieces(l_ref[...], 2) + [jnp.zeros((3, 640), F32)], axis=0
    )
    for o in range(2):
        for k in range(8):
            at = slice(o * 320 + k * 40, o * 320 + k * 40 + 40)
            tail = jnp.concatenate([stats[:, at], jnp.zeros((8, 88), F32)], axis=1)
            msg[o, k] = jnp.concatenate([sums_rows[at], tail], axis=0).astype(BF)
    parts = [None] * 16
    for k in (12, 4, 11, 13, 3, 5, 10, 14, 2, 6, 9, 15, 1, 7, 8):
        dh, dz = column[k]
        parts[k] = send(msg.at[dh, (z + dz) % 8], accr.at[k], ac_s.at[k], ac_r.at[k], in_column(k))
    accr[0] = msg[0, z]

    pass_weights_on()
    for k in range(1, 16):
        parts[k].wait_recv()
    stats = accr[:, 32:48, :].astype(F32)
    tops = stats[:, 8] + stats[:, 9] + stats[:, 10]
    sums = stats[:, 11] + stats[:, 12]
    factor = jnp.exp2(tops - jnp.max(tops, axis=0, keepdims=True))
    factor = (factor / jnp.sum(factor * sums, axis=0, keepdims=True)).T
    total = jnp.zeros((48, 128), F32)
    for k in range(16):
        total = total + accr[k].astype(F32) * factor[0:48, k : k + 1]
    attp[...] = total.astype(BF)

    gathered = [None] * 8
    for dz in (4, 3, 5, 2, 6, 1, 7):
        gathered[dz] = send(attp, att_g.at[z], at_s.at[dz], at_r.at[dz], in_column(dz))
    att_g[z] = attp[...]
    pass_crossed_weights_on()
    for k in range(4):
        w_fwd[k].wait_recv()
    for dz in range(1, 8):
        gathered[dz].wait_recv()

    att = att_g[...].astype(F32)[:, :40].reshape(320, 128).astype(BF)
    proj = jnp.zeros((64, 640), F32)
    for i in range(5):
        proj += jnp.dot(att[i * 64 : i * 64 + 64], wb[i * 128 : i * 128 + 128, :], preferred_element_type=F32)
    for k in range(8):
        os[k] = jnp.concatenate([proj[:, 80 * k : 80 * k + 80], jnp.zeros((64, 48), F32)], axis=1).astype(BF)
    outs = [None] * 8
    for j in (7, 6, 5, 4, 3, 2, 1):
        dm, dy = plane[j]
        k = 2 * ((y + dy) % 4) + ((m + dm) % 2 + h) % 2
        outs[j] = send(os.at[k], orv.at[j], o_s.at[j], o_r.at[j], in_plane(j))
    result = os[2 * y + l].astype(F32)
    for j in range(1, 8):
        outs[j].wait_recv()
        result += orv[j].astype(F32)
    out_ref[...] = result[:, :80].astype(BF)

    finish()


def on_device(queries, fresh_kv, kv_pages, page_list, tile_mask, out_weight):
    hbm, vmem = pl.BlockSpec(memory_space=pltpu.HBM), pl.BlockSpec(memory_space=pltpu.VMEM)
    sem = lambda n: pltpu.SemaphoreType.DMA((n,))
    out = pl.pallas_call(
        kernel,
        out_shape=jax.ShapeDtypeStruct((64, 80), BF),
        in_specs=[hbm] * 6,
        out_specs=vmem,
        scratch_shapes=[
            pltpu.VMEM((4, 64), jnp.int32),
            pltpu.VMEM((4, 64), jnp.int32),
            pltpu.VMEM((2, 64, 640), BF),
            pltpu.VMEM((640, 128), BF),
            pltpu.VMEM((2, 16, 128, 128), BF),
            pltpu.VMEM((2, 64, 128), BF),
            pltpu.VMEM((2, 8, 128), jnp.int32),
            pltpu.VMEM((16, 640), F32),
            pltpu.VMEM((1, 640), F32),
            pltpu.VMEM((1, 640), F32),
            pltpu.VMEM((128, 640), F32),
            pltpu.VMEM((80, 5120), BF),
            pltpu.VMEM((8, 80, 640), BF),
            pltpu.VMEM((640, 640), BF),
            pltpu.VMEM((2, 8, 48, 128), BF),
            pltpu.VMEM((16, 48, 128), BF),
            pltpu.VMEM((48, 128), BF),
            pltpu.VMEM((8, 48, 128), BF),
            pltpu.VMEM((8, 64, 128), BF),
            pltpu.VMEM((8, 64, 128), BF),
            sem(7), sem(8), sem(8), sem(8), sem(8), sem(2), sem(2), sem(4), sem(2), sem(2), sem(2), sem(4), sem(4),
            sem(16), sem(16), sem(8), sem(8), sem(8), sem(8),
        ],
        compiler_params=pltpu.CompilerParams(
            collective_id=0, has_side_effects=True, vmem_limit_bytes=62 * 2**20
        ),
        name="attend",
    )(
        queries.reshape(64, 5120),
        fresh_kv.reshape(2, 64, 1024),
        kv_pages.reshape(2, 128, 1024),
        page_list,
        tile_mask,
        out_weight,
    )
    return out.reshape(4, 16, 80)


def solution(mesh):
    return jax.shard_map(
        on_device,
        mesh=mesh,
        in_specs=(
            P("group", None, None),
            P(None, "group", None, None),
            P(None, ("group", "shard"), None, None),
            P("group", None),
            P("group", None),
            P("shard", None),
        ),
        out_specs=P("group", None, "shard"),
        check_vma=False,
    )
```

```python
import functools
import math

import jax
import jax.numpy as jnp
from jax import lax
from jax.experimental import pallas as pl
from jax.experimental.pallas import tpu as pltpu
from jax.sharding import PartitionSpec as P

MESH = pl.DeviceIdType.MESH
BF, F32 = jnp.bfloat16, jnp.float32
HIDDEN = -1e30
FLOOR = -1e29
FAR_FIRST = (12, 4, 11, 13, 3, 5, 10, 14, 2, 6, 9, 15, 1, 7, 8)


def device(h, m, y, z, c):
    return (h * 2 + c, (y * 8 + z) * 2 + (m + h) % 2)


def kernel(
    q_hbm, f_hbm, kv_hbm, list_hbm, mask_hbm, w_hbm, out_ref,
    list_ref, mask_ref, qb, qc, kvb, fb, eb, bias, m_ref, l_ref, acc, wv, wp, wb,
    msg, accr, attp, att_g, os, orv,
    loc, pg_s, pg_r, fw_s, fw_r, q_s, q_r, w_s, w_r, wx_s, wx_r,
    ac_s, ac_r, at_s, at_r, o_s, o_r,
):
    g = lax.axis_index("group")
    s = lax.axis_index("shard")
    h, c = g // 2, g % 2
    y, z, l = s // 16, (s // 2) % 8, s % 2
    m = (l + h) % 2
    head = 2 * y + m
    plane = [(0, 0), (1, 0), (0, 1), (0, 3), (1, 1), (1, 3), (0, 2), (1, 2)]
    column = [(dh, dz) for dh in range(2) for dz in range(8)]
    sibling = device(h, m, y, z, 1 - c)
    across = device(1 - h, m, y, z, c)

    def in_plane(j, core):
        dm, dy = plane[j]
        return device(h, (m + dm) % 2, (y + dy) % 4, z, core)

    def in_column(k, core):
        dh, dz = column[k]
        return device((h + dh) % 2, m, y, (z + dz) % 8, core)

    holder = z // 4 == m
    w_to = [2 * k + (z + c) % 2 for k in range(4)]

    def w_rows(zz, ll):
        return pl.ds(pl.multiple_of(80 * ((zz % 4) * 2 + ll), 16), 80)

    bar = pltpu.get_barrier_semaphore()

    def greet(d):
        pl.semaphore_signal(bar, inc=1, device_id=d, device_id_type=MESH)

    @pl.when(c == 1)
    def _():
        for k in FAR_FIRST:
            greet(in_column(k, 1))
            greet(in_column(k, 0))
        for j in range(7, 0, -1):
            greet(in_plane(j, 1))

    for j in range(7, 0, -1):
        greet(in_plane(j, 1 - c))
    greet(sibling)
    pl.when(c == 0)(lambda: greet(across))

    cols = pl.ds(pl.multiple_of(head * 128, 128), 128)
    q_cols = pl.ds(pl.multiple_of(head * 640, 128), 640)
    ld_q = pltpu.make_async_copy(q_hbm.at[:, q_cols], qb.at[0], loc.at[0])
    ld_kv = pltpu.make_async_copy(kv_hbm.at[:, :, cols], kvb.at[:, 0], loc.at[1])
    ld_f = pltpu.make_async_copy(f_hbm.at[:, :, cols], fb, loc.at[2])
    ld_w = pltpu.make_async_copy(w_hbm, wv, loc.at[3])
    ld_list = pltpu.make_async_copy(list_hbm, list_ref, loc.at[5])
    ld_mask = pltpu.make_async_copy(mask_hbm, mask_ref, loc.at[6])
    for ld in (ld_list, ld_mask, ld_q, ld_kv, ld_w, ld_f):
        ld.start()

    eb[0] = jnp.full((8, 128), -1, jnp.int32)
    ld_list.wait()
    ld_mask.wait()
    eb[0, 0:4, 0:64] = jnp.where(mask_ref[...] > 0, list_ref[...], -1)

    ld_w.wait()
    for z2 in range(8):
        wp[z2] = jnp.concatenate(
            [wv[:, 1280 * y2 + 160 * z2 : 1280 * y2 + 160 * z2 + 160] for y2 in range(4)], axis=1
        )

    pl.semaphore_wait(bar, 24 + 6 * c)

    def send(src, dst, ss, rs, d):
        cp = pltpu.make_async_remote_copy(
            src_ref=src, dst_ref=dst, send_sem=ss, recv_sem=rs, device_id=d, device_id_type=MESH
        )
        cp.start()
        pending.append(cp)
        return cp

    def forward(j):
        return pltpu.make_async_remote_copy(
            src_ref=kvb.at[:, j], dst_ref=kvb.at[:, 8 + j], send_sem=fw_s.at[j], recv_sem=fw_r.at[j],
            device_id=sibling, device_id_type=MESH,
        )

    def pages_in(j):
        return pltpu.make_async_remote_copy(
            src_ref=kvb.at[:, 0], dst_ref=kvb.at[:, j], send_sem=pg_s.at[j], recv_sem=pg_r.at[j],
            device_id=sibling, device_id_type=MESH,
        )

    pending = []
    snd_e = send(eb.at[0], eb.at[1], q_s.at[0], q_r.at[0], across)
    for j in range(1, 8):
        dm, dy = plane[j]
        there = 2 * ((y + dy) % 4) + (m + dm) % 2
        there_cols = pl.ds(pl.multiple_of(there * 128, 128), 128)
        send(kv_hbm.at[:, :, there_cols], kvb.at[:, j], pg_s.at[j], pg_r.at[j], in_plane(j, 1 - c))
    ld_q.wait()
    snd_q = send(qb.at[0], qb.at[1], q_s.at[1], q_r.at[1], across)
    ld_kv.wait()

    forward(0).start()

    def w_send(k):
        return pltpu.make_async_remote_copy(
            src_ref=wp.at[w_to[k]], dst_ref=wb.at[w_rows(z, l)], send_sem=w_s.at[k], recv_sem=w_r.at[z % 4],
            device_id=device(h, m, y, w_to[k], 1), device_id_type=MESH,
        )

    def w_cross(k):
        rows = wb.at[w_rows(k, l)]
        return pltpu.make_async_remote_copy(
            src_ref=rows, dst_ref=rows, send_sem=wx_s.at[k], recv_sem=wx_r.at[k], device_id=across, device_id_type=MESH
        )

    for k in range(4):
        pl.when(holder)(lambda: w_send(k).start())

    def w_pass_on(k):
        pltpu.make_async_remote_copy(
            src_ref=wp.at[0], dst_ref=wb.at[w_rows(k, l)], send_sem=w_s.at[k], recv_sem=w_r.at[k],
            device_id=across, device_id_type=MESH,
        ).wait_recv()
        w_cross(k).start()

    snd_e.wait_recv()
    lists = eb[...].reshape(16, 128)
    row = lax.broadcasted_iota(jnp.int32, (16, 640), 0)
    col = lax.broadcasted_iota(jnp.int32, (16, 640), 1)
    owner = jnp.where(col >= 320, 8, 0) + ((col >> 4) & 3)
    pick = (row == owner).astype(F32)
    for j in range(16):
        dm, dy = plane[j % 8]
        src_m, src_y, src_c = (m - dm + 2) % 2, (y - dy + 4) % 4, (c + j // 8 + min(j % 8, 1)) % 2
        src_l = (src_m + h) % 2
        number = (h * 2 + src_c) * 64 + (src_y * 8 + z) * 2 + src_l
        seen = jnp.max((lists == number).astype(F32), axis=1, keepdims=True)
        bias[j] = (jnp.sum(pick * seen, axis=0, keepdims=True) - 1.0) * (-HIDDEN)

    snd_q.wait_recv()
    for o in range(2):
        for i in range(5):
            qc[o * 320 + i * 64 : o * 320 + i * 64 + 64, :] = qb[o, :, i * 128 : i * 128 + 128]

    scale = math.log2(math.e) / math.sqrt(128)

    def scores(keys):
        return lax.dot_general(keys, qc[...], (((1,), (1,)), ((), ())), preferred_element_type=F32) * scale

    def weigh(values, weights):
        return lax.dot_general(
            values, weights.astype(BF), (((0,), (0,)), ((), ())), preferred_element_type=F32
        )

    ld_f.wait()
    key = lax.broadcasted_iota(jnp.int32, (64, 640), 0)
    col = lax.broadcasted_iota(jnp.int32, (64, 640), 1)
    visible = (col < 320) & ((key >> 4) == ((col >> 4) & 3)) & ((key & 15) <= (col & 15)) & (z == 0)
    sc = jnp.where(visible, scores(fb[0]), HIDDEN)
    top = jnp.maximum(jnp.max(sc, axis=0, keepdims=True), FLOOR)
    wt = jnp.exp2(sc - top)
    m_ref[...] = top
    l_ref[...] = jnp.sum(wt, axis=0, keepdims=True)
    acc[...] = weigh(fb[1], wt)

    @pl.loop(0, 4)
    def _(n):
        @pl.when(n % 2 == 0)
        def _():
            for j in range(4):
                @pl.when(n + j > 0)
                def _():
                    pages_in(2 * n + j).wait_recv()
                    forward(2 * n + j).start()

        @pl.when(n % 2 == 1)
        def _():
            for j in range(4):
                forward(2 * (n - 1) + j).wait_recv()

        first = (n % 2) * 8 + (n // 2) * 4
        slots = pl.ds(first, 4)
        sc = scores(kvb[0, slots].reshape(512, 128))
        sc = (sc.reshape(4, 128, 640) + bias[slots]).reshape(512, 640)
        old = m_ref[...]
        top = jnp.maximum(old, jnp.max(sc, axis=0, keepdims=True))
        keep = jnp.exp2(old - top)
        wt = jnp.exp2(sc - top)
        m_ref[...] = top
        l_ref[...] = l_ref[...] * keep + jnp.sum(wt, axis=0, keepdims=True)
        acc[...] = acc[...] * keep + weigh(kvb[1, slots].reshape(512, 128), wt)

    def pieces(x, n):
        out = []
        for _ in range(n):
            out.append(x.astype(BF).astype(F32))
            x = x - out[-1]
        return out

    sums_rows = acc[...].T
    stats = jnp.concatenate(
        pieces(m_ref[...], 3) + pieces(l_ref[...], 2) + [jnp.zeros((3, 640), F32)], axis=0
    )
    for o in range(2):
        for k in range(8):
            at = slice(o * 320 + k * 40, o * 320 + k * 40 + 40)
            tail = jnp.concatenate([stats[:, at], jnp.zeros((8, 88), F32)], axis=1)
            msg[o, k] = jnp.concatenate([sums_rows[at], tail], axis=0).astype(BF)
    def part(k):
        dh, dz = column[k]
        return pltpu.make_async_remote_copy(
            src_ref=msg.at[dh, (z + dz) % 8], dst_ref=accr.at[c * 16 + k], send_sem=ac_s.at[k], recv_sem=ac_r.at[c * 16 + k],
            device_id=in_column(k, 1), device_id_type=MESH,
        )

    def part_in(i):
        return pltpu.make_async_remote_copy(
            src_ref=msg.at[0, 0], dst_ref=accr.at[i], send_sem=ac_s.at[0], recv_sem=ac_r.at[i],
            device_id=sibling, device_id_type=MESH,
        )

    def piece_to(dz):
        return pltpu.make_async_remote_copy(
            src_ref=attp, dst_ref=att_g.at[z], send_sem=at_s.at[dz], recv_sem=at_r.at[dz],
            device_id=in_column(dz, 1), device_id_type=MESH,
        )

    def out_to(j, core):
        dm, dy = plane[j]
        k = 2 * ((y + dy) % 4) + ((m + dm) % 2 + h) % 2
        return pltpu.make_async_remote_copy(
            src_ref=os.at[k, core], dst_ref=orv.at[j], send_sem=o_s.at[core * 8 + j], recv_sem=o_r.at[j],
            device_id=in_plane(j, core), device_id_type=MESH,
        )

    for k in FAR_FIRST:
        part(k).start()
    pl.when(c == 0)(lambda: part(0).start())

    @pl.when(c == 1)
    def _():
        accr[16] = msg[0, z]
        for k in range(4):
            w_pass_on(k)
        for i in range(32):
            if i != 16:
                part_in(i).wait_recv()
        for i in range(2):
            ours = slice(16 * i, 16 * i + 16)
            stats = accr[ours, 32:48, :].astype(F32)
            tops = stats[:, 8] + stats[:, 9] + stats[:, 10]
            sums = stats[:, 11] + stats[:, 12]
            factor = jnp.exp2(tops - jnp.max(tops, axis=0, keepdims=True))
            factor = (factor / jnp.sum(factor * sums, axis=0, keepdims=True)).T
            total = jnp.zeros((48, 128), F32)
            for k in range(16):
                total = total + accr[16 * i + k].astype(F32) * factor[0:48, k : k + 1]
            attp[i] = total.astype(BF)
        for dz in (4, 3, 5, 2, 6, 1, 7):
            piece_to(dz).start()
        att_g[z] = attp[...]
        for k in range(4):
            pltpu.make_async_remote_copy(
                src_ref=wp.at[0], dst_ref=wb.at[w_rows(k, 1 - l)], send_sem=wx_s.at[k], recv_sem=wx_r.at[k],
                device_id=across, device_id_type=MESH,
            ).wait_recv()
        for dz in range(1, 8):
            pltpu.make_async_remote_copy(
                src_ref=attp, dst_ref=att_g.at[(z - dz + 8) % 8], send_sem=at_s.at[dz], recv_sem=at_r.at[dz],
                device_id=sibling, device_id_type=MESH,
            ).wait_recv()
        att = [att_g[:, i].astype(F32)[:, :40].reshape(320, 128).astype(BF) for i in range(2)]
        proj = jnp.zeros((128, 640), F32)
        for i in range(5):
            rows = slice(i * 64, i * 64 + 64)
            proj += jnp.dot(
                jnp.concatenate([att[0][rows], att[1][rows]], axis=0), wb[i * 128 : i * 128 + 128, :],
                preferred_element_type=F32,
            )
        for k in range(8):
            chunk = jnp.concatenate([proj[:, 80 * k : 80 * k + 80], jnp.zeros((128, 48), F32)], axis=1)
            os[k] = chunk.astype(BF).reshape(2, 64, 128)
        for j in range(7, -1, -1):
            out_to(j, 0).start()
            if j:
                out_to(j, 1).start()
        orv[0] = os[2 * y + l, 1]

    result = jnp.zeros((64, 128), F32)
    pl.when(c == 0)(lambda: out_to(0, 0).wait_recv())
    for j in range(7, -1, -1):
        if j:
            out_to(j, 0).wait_recv()
        result += orv[j].astype(F32)
    out_ref[...] = result[:, :80].astype(BF)

    for cp in pending:
        cp.wait_send()
    for j in range(8):
        forward(j).wait_send()
    for k in range(4):
        pl.when(holder)(lambda: w_send(k).wait_send())
    for k in FAR_FIRST:
        part(k).wait_send()
    pl.when(c == 0)(lambda: part(0).wait_send())

    @pl.when(c == 1)
    def _():
        for k in range(4):
            w_cross(k).wait_send()
        for dz in range(1, 8):
            piece_to(dz).wait_send()
        for j in range(8):
            out_to(j, 0).wait_send()
            if j:
                out_to(j, 1).wait_send()


def on_device(queries, fresh_kv, kv_pages, page_list, tile_mask, out_weight):
    hbm, vmem = pl.BlockSpec(memory_space=pltpu.HBM), pl.BlockSpec(memory_space=pltpu.VMEM)
    sem = lambda n: pltpu.SemaphoreType.DMA((n,))
    out = pl.pallas_call(
        kernel,
        out_shape=jax.ShapeDtypeStruct((64, 80), BF),
        in_specs=[hbm] * 6,
        out_specs=vmem,
        scratch_shapes=[
            pltpu.VMEM((4, 64), jnp.int32),
            pltpu.VMEM((4, 64), jnp.int32),
            pltpu.VMEM((2, 64, 640), BF),
            pltpu.VMEM((640, 128), BF),
            pltpu.VMEM((2, 16, 128, 128), BF),
            pltpu.VMEM((2, 64, 128), BF),
            pltpu.VMEM((2, 8, 128), jnp.int32),
            pltpu.VMEM((16, 1, 640), F32),
            pltpu.VMEM((1, 640), F32),
            pltpu.VMEM((1, 640), F32),
            pltpu.VMEM((128, 640), F32),
            pltpu.VMEM((80, 5120), BF),
            pltpu.VMEM((8, 80, 640), BF),
            pltpu.VMEM((640, 640), BF),
            pltpu.VMEM((2, 8, 48, 128), BF),
            pltpu.VMEM((32, 48, 128), BF),
            pltpu.VMEM((2, 48, 128), BF),
            pltpu.VMEM((8, 2, 48, 128), BF),
            pltpu.VMEM((8, 2, 64, 128), BF),
            pltpu.VMEM((8, 64, 128), BF),
            sem(7), sem(8), sem(8), sem(8), sem(8), sem(2), sem(2), sem(4), sem(4), sem(4), sem(4),
            sem(16), sem(32), sem(8), sem(8), sem(16), sem(8),
        ],
        compiler_params=pltpu.CompilerParams(
            collective_id=0, has_side_effects=True, vmem_limit_bytes=int(53.9 * 2**20)
        ),
        name="attend",
    )(
        queries.reshape(64, 5120),
        fresh_kv.reshape(2, 64, 1024),
        kv_pages.reshape(2, 128, 1024),
        page_list,
        tile_mask,
        out_weight,
    )
    return out.reshape(4, 16, 80)


def solution(mesh):
    return jax.shard_map(
        on_device,
        mesh=mesh,
        in_specs=(
            P("group", None, None),
            P(None, "group", None, None),
            P(None, ("group", "shard"), None, None),
            P("group", None),
            P("group", None),
            P("shard", None),
        ),
        out_specs=P("group", None, "shard"),
        check_vma=False,
    )
```

```python
import functools
import math

import jax
import jax.numpy as jnp
from jax import lax
from jax.experimental import pallas as pl
from jax.experimental.pallas import tpu as pltpu
from jax.sharding import PartitionSpec as P

MESH = pl.DeviceIdType.MESH
BF, F32 = jnp.bfloat16, jnp.float32
HIDDEN = -1e30
FLOOR = -1e29
FAR_FIRST = (12, 4, 11, 13, 3, 5, 10, 14, 2, 6, 9, 15, 1, 7, 8)


def device(h, m, y, z, c):
    return (h * 2 + c, (y * 8 + z) * 2 + (m + h) % 2)


def kernel(
    q_hbm, f_hbm, kv_hbm, list_hbm, mask_hbm, w_hbm, out_ref,
    list_ref, mask_ref, qb, qc, kvb, fb, eb, bias, m_ref, l_ref, acc, wv, wp, wb,
    msg, accr, attp, att_g, os, orv,
    loc, pg_s, pg_r, fw_s, fw_r, q_s, q_r, w_s, w_r, wx_s, wx_r,
    ac_s, ac_r, at_s, at_r, o_s, o_r,
):
    g = lax.axis_index("group")
    s = lax.axis_index("shard")
    h, c = g // 2, g % 2
    y, z, l = s // 16, (s // 2) % 8, s % 2
    m = (l + h) % 2
    head = 2 * y + m
    plane = [(0, 0), (1, 0), (0, 1), (0, 3), (1, 1), (1, 3), (0, 2), (1, 2)]
    column = [(dh, dz) for dh in range(2) for dz in range(8)]
    sibling = device(h, m, y, z, 1 - c)
    across = device(1 - h, m, y, z, c)

    def in_plane(j, core):
        dm, dy = plane[j]
        return device(h, (m + dm) % 2, (y + dy) % 4, z, core)

    def in_column(k, core):
        dh, dz = column[k]
        return device((h + dh) % 2, m, y, (z + dz) % 8, core)

    holder = z // 4 == m
    w_to = [2 * k + (z + c) % 2 for k in range(4)]

    def w_rows(zz, ll):
        return pl.ds(pl.multiple_of(80 * ((zz % 4) * 2 + ll), 16), 80)

    bar = pltpu.get_barrier_semaphore()

    def greet(d):
        pl.semaphore_signal(bar, inc=1, device_id=d, device_id_type=MESH)

    @pl.when(c == 1)
    def _():
        for k in FAR_FIRST:
            greet(in_column(k, 1))
            greet(in_column(k, 0))
        for j in range(7, 0, -1):
            greet(in_plane(j, 1))

    for j in range(7, 0, -1):
        greet(in_plane(j, 1 - c))
    greet(sibling)
    pl.when(c == 0)(lambda: greet(across))

    cols = pl.ds(pl.multiple_of(head * 128, 128), 128)
    q_cols = pl.ds(pl.multiple_of(head * 640, 128), 640)
    ld_q = pltpu.make_async_copy(q_hbm.at[:, q_cols], qb.at[0], loc.at[0])
    ld_kv = pltpu.make_async_copy(kv_hbm.at[:, :, cols], kvb.at[:, 0], loc.at[1])
    ld_f = pltpu.make_async_copy(f_hbm.at[:, :, cols], fb, loc.at[2])
    ld_w = pltpu.make_async_copy(w_hbm, wv, loc.at[3])
    ld_list = pltpu.make_async_copy(list_hbm, list_ref, loc.at[5])
    ld_mask = pltpu.make_async_copy(mask_hbm, mask_ref, loc.at[6])
    for ld in (ld_list, ld_mask, ld_q, ld_kv, ld_w, ld_f):
        ld.start()

    pl.semaphore_wait(bar, 24 + 6 * c)

    def send(src, dst, ss, rs, d):
        cp = pltpu.make_async_remote_copy(
            src_ref=src, dst_ref=dst, send_sem=ss, recv_sem=rs, device_id=d, device_id_type=MESH
        )
        cp.start()
        pending.append(cp)
        return cp

    def forward(j):
        return pltpu.make_async_remote_copy(
            src_ref=kvb.at[:, j], dst_ref=kvb.at[:, 8 + j], send_sem=fw_s.at[j], recv_sem=fw_r.at[j],
            device_id=sibling, device_id_type=MESH,
        )

    def pages_in(j):
        return pltpu.make_async_remote_copy(
            src_ref=kvb.at[:, 0], dst_ref=kvb.at[:, j], send_sem=pg_s.at[j], recv_sem=pg_r.at[j],
            device_id=sibling, device_id_type=MESH,
        )

    pending = []
    for j in range(1, 8):
        dm, dy = plane[j]
        there = 2 * ((y + dy) % 4) + (m + dm) % 2
        there_cols = pl.ds(pl.multiple_of(there * 128, 128), 128)
        send(kv_hbm.at[:, :, there_cols], kvb.at[:, j], pg_s.at[j], pg_r.at[j], in_plane(j, 1 - c))
    eb[0] = jnp.full((8, 128), -1, jnp.int32)
    ld_list.wait()
    ld_mask.wait()
    eb[0, 0:4, 0:64] = jnp.where(mask_ref[...] > 0, list_ref[...], -1)
    snd_e = send(eb.at[0], eb.at[1], q_s.at[0], q_r.at[0], across)
    ld_q.wait()
    snd_q = send(qb.at[0], qb.at[1], q_s.at[1], q_r.at[1], across)
    ld_kv.wait()

    forward(0).start()

    ld_w.wait()
    for z2 in range(8):
        wp[z2] = jnp.concatenate(
            [wv[:, 1280 * y2 + 160 * z2 : 1280 * y2 + 160 * z2 + 160] for y2 in range(4)], axis=1
        )

    def w_send(k):
        return pltpu.make_async_remote_copy(
            src_ref=wp.at[w_to[k]], dst_ref=wb.at[w_rows(z, l)], send_sem=w_s.at[k], recv_sem=w_r.at[z % 4],
            device_id=device(h, m, y, w_to[k], 1), device_id_type=MESH,
        )

    def w_cross(k):
        rows = wb.at[w_rows(k, l)]
        return pltpu.make_async_remote_copy(
            src_ref=rows, dst_ref=rows, send_sem=wx_s.at[k], recv_sem=wx_r.at[k], device_id=across, device_id_type=MESH
        )

    for k in range(4):
        pl.when(holder)(lambda: w_send(k).start())

    def w_pass_on(k):
        pltpu.make_async_remote_copy(
            src_ref=wp.at[0], dst_ref=wb.at[w_rows(k, l)], send_sem=w_s.at[k], recv_sem=w_r.at[k],
            device_id=across, device_id_type=MESH,
        ).wait_recv()
        w_cross(k).start()

    snd_e.wait_recv()
    lists = eb[...].reshape(16, 128)
    row = lax.broadcasted_iota(jnp.int32, (16, 640), 0)
    col = lax.broadcasted_iota(jnp.int32, (16, 640), 1)
    owner = jnp.where(col >= 320, 8, 0) + ((col >> 4) & 3)
    pick = (row == owner).astype(F32)
    for j in range(16):
        dm, dy = plane[j % 8]
        src_m, src_y, src_c = (m - dm + 2) % 2, (y - dy + 4) % 4, (c + j // 8 + min(j % 8, 1)) % 2
        src_l = (src_m + h) % 2
        number = (h * 2 + src_c) * 64 + (src_y * 8 + z) * 2 + src_l
        seen = jnp.max((lists == number).astype(F32), axis=1, keepdims=True)
        bias[j] = (jnp.sum(pick * seen, axis=0, keepdims=True) - 1.0) * (-HIDDEN)

    snd_q.wait_recv()
    for o in range(2):
        for i in range(5):
            qc[o * 320 + i * 64 : o * 320 + i * 64 + 64, :] = qb[o, :, i * 128 : i * 128 + 128]

    scale = math.log2(math.e) / math.sqrt(128)

    def scores(keys):
        return lax.dot_general(keys, qc[...], (((1,), (1,)), ((), ())), preferred_element_type=F32) * scale

    def weigh(values, weights):
        return lax.dot_general(
            values, weights.astype(BF), (((0,), (0,)), ((), ())), preferred_element_type=F32
        )

    ld_f.wait()
    key = lax.broadcasted_iota(jnp.int32, (64, 640), 0)
    col = lax.broadcasted_iota(jnp.int32, (64, 640), 1)
    visible = (col < 320) & ((key >> 4) == ((col >> 4) & 3)) & ((key & 15) <= (col & 15)) & (z == 0)
    sc = jnp.where(visible, scores(fb[0]), HIDDEN)
    top = jnp.maximum(jnp.max(sc, axis=0, keepdims=True), FLOOR)
    wt = jnp.exp2(sc - top)
    m_ref[...] = top
    l_ref[...] = jnp.sum(wt, axis=0, keepdims=True)
    acc[...] = weigh(fb[1], wt)

    @pl.loop(0, 4)
    def _(n):
        @pl.when(n % 2 == 0)
        def _():
            for j in range(4):
                @pl.when(n + j > 0)
                def _():
                    pages_in(2 * n + j).wait_recv()
                    forward(2 * n + j).start()

        @pl.when(n % 2 == 1)
        def _():
            for j in range(4):
                forward(2 * (n - 1) + j).wait_recv()

        first = (n % 2) * 8 + (n // 2) * 4
        slots = pl.ds(first, 4)
        sc = scores(kvb[0, slots].reshape(512, 128))
        sc = (sc.reshape(4, 128, 640) + bias[slots]).reshape(512, 640)
        old = m_ref[...]
        top = jnp.maximum(old, jnp.max(sc, axis=0, keepdims=True))
        keep = jnp.exp2(old - top)
        wt = jnp.exp2(sc - top)
        m_ref[...] = top
        l_ref[...] = l_ref[...] * keep + jnp.sum(wt, axis=0, keepdims=True)
        acc[...] = acc[...] * keep + weigh(kvb[1, slots].reshape(512, 128), wt)

    def pieces(x, n):
        out = []
        for _ in range(n):
            out.append(x.astype(BF).astype(F32))
            x = x - out[-1]
        return out

    sums_rows = acc[...].T
    stats = jnp.concatenate(
        pieces(m_ref[...], 3) + pieces(l_ref[...], 2) + [jnp.zeros((3, 640), F32)], axis=0
    )
    def fill(o):
        for k in range(8):
            at = slice(o * 320 + k * 40, o * 320 + k * 40 + 40)
            tail = jnp.concatenate([stats[:, at], jnp.zeros((8, 88), F32)], axis=1)
            msg[o, k] = jnp.concatenate([sums_rows[at], tail], axis=0).astype(BF)

    def part(half, dz):
        dh = (half + h) % 2
        k = dh * 8 + dz
        return pltpu.make_async_remote_copy(
            src_ref=msg.at[dh, (z + dz) % 8], dst_ref=accr.at[c * 16 + k], send_sem=ac_s.at[k], recv_sem=ac_r.at[c * 16 + k],
            device_id=device(half, m, y, (z + dz) % 8, 1), device_id_type=MESH,
        )

    def part_in(i):
        return pltpu.make_async_remote_copy(
            src_ref=msg.at[0, 0], dst_ref=accr.at[i], send_sem=ac_s.at[0], recv_sem=ac_r.at[i],
            device_id=sibling, device_id_type=MESH,
        )

    def piece_to(dz):
        return pltpu.make_async_remote_copy(
            src_ref=attp, dst_ref=att_g.at[z], send_sem=at_s.at[dz], recv_sem=at_r.at[dz],
            device_id=in_column(dz, 1), device_id_type=MESH,
        )

    def out_to(j, core):
        dm, dy = plane[j]
        k = 2 * ((y + dy) % 4) + ((m + dm) % 2 + h) % 2
        return pltpu.make_async_remote_copy(
            src_ref=os.at[k, core], dst_ref=orv.at[j], send_sem=o_s.at[core * 8 + j], recv_sem=o_r.at[j],
            device_id=in_plane(j, core), device_id_type=MESH,
        )

    fill(0)
    fill(1)
    others = [(half, dz) for dz in (4, 3, 5, 2, 6, 1, 7) for half in range(2)] + [(1 - h, 0)]
    for half, dz in others:
        part(half, dz).start()
    pl.when(c == 0)(lambda: part(h, 0).start())

    @pl.when(c == 1)
    def _():
        accr[16] = msg[0, z]
        for k in range(4):
            w_pass_on(k)
        for i in range(32):
            if i != 16:
                part_in(i).wait_recv()
        stats = accr[:, 32:48, :].astype(F32)
        tops = (stats[:, 8] + stats[:, 9] + stats[:, 10]).reshape(2, 16, 128)
        sums = (stats[:, 11] + stats[:, 12]).reshape(2, 16, 128)
        factor = jnp.exp2(tops - jnp.max(tops, axis=1, keepdims=True))
        factor = (factor / jnp.sum(factor * sums, axis=1, keepdims=True)).reshape(32, 128).T
        for i in range(2):
            total = jnp.zeros((40, 128), F32)
            for k in range(16 * i, 16 * i + 16):
                total = total + accr[k, 0:40].astype(F32) * factor[0:40, k : k + 1]
            attp[i] = jnp.concatenate([total, jnp.zeros((8, 128), F32)], axis=0).astype(BF)
        for dz in (4, 3, 5, 2, 6, 1, 7):
            piece_to(dz).start()
        att_g[z] = attp[...]
        for k in range(4):
            pltpu.make_async_remote_copy(
                src_ref=wp.at[0], dst_ref=wb.at[w_rows(k, 1 - l)], send_sem=wx_s.at[k], recv_sem=wx_r.at[k],
                device_id=across, device_id_type=MESH,
            ).wait_recv()
        for dz in range(1, 8):
            pltpu.make_async_remote_copy(
                src_ref=attp, dst_ref=att_g.at[(z - dz + 8) % 8], send_sem=at_s.at[dz], recv_sem=at_r.at[dz],
                device_id=sibling, device_id_type=MESH,
            ).wait_recv()
        att = [att_g[:, i].astype(F32)[:, :40].reshape(320, 128).astype(BF) for i in range(2)]
        proj = jnp.zeros((128, 640), F32)
        for i in range(5):
            rows = slice(i * 64, i * 64 + 64)
            proj += jnp.dot(
                jnp.concatenate([att[0][rows], att[1][rows]], axis=0), wb[i * 128 : i * 128 + 128, :],
                preferred_element_type=F32,
            )
        proj = proj.astype(BF)
        for k in range(8):
            for i in range(2):
                os[k, i, :, 0:80] = proj[64 * i : 64 * i + 64, 80 * k : 80 * k + 80]
        for j in range(7, -1, -1):
            out_to(j, 0).start()
            if j:
                out_to(j, 1).start()
        orv[0] = os[2 * y + l, 1]

    result = jnp.zeros((64, 128), F32)
    pl.when(c == 0)(lambda: out_to(0, 0).wait_recv())
    for j in range(7, -1, -1):
        if j:
            out_to(j, 0).wait_recv()
        result += orv[j].astype(F32)
    out_ref[...] = result[:, :80].astype(BF)

    for cp in pending:
        cp.wait_send()
    for j in range(8):
        forward(j).wait_send()
    for k in range(4):
        pl.when(holder)(lambda: w_send(k).wait_send())
    for half, dz in others:
        part(half, dz).wait_send()
    pl.when(c == 0)(lambda: part(h, 0).wait_send())

    @pl.when(c == 1)
    def _():
        for k in range(4):
            w_cross(k).wait_send()
        for dz in range(1, 8):
            piece_to(dz).wait_send()
        for j in range(8):
            out_to(j, 0).wait_send()
            if j:
                out_to(j, 1).wait_send()


def on_device(queries, fresh_kv, kv_pages, page_list, tile_mask, out_weight):
    hbm, vmem = pl.BlockSpec(memory_space=pltpu.HBM), pl.BlockSpec(memory_space=pltpu.VMEM)
    sem = lambda n: pltpu.SemaphoreType.DMA((n,))
    out = pl.pallas_call(
        kernel,
        out_shape=jax.ShapeDtypeStruct((64, 80), BF),
        in_specs=[hbm] * 6,
        out_specs=vmem,
        scratch_shapes=[
            pltpu.VMEM((4, 64), jnp.int32),
            pltpu.VMEM((4, 64), jnp.int32),
            pltpu.VMEM((2, 64, 640), BF),
            pltpu.VMEM((640, 128), BF),
            pltpu.VMEM((2, 16, 128, 128), BF),
            pltpu.VMEM((2, 64, 128), BF),
            pltpu.VMEM((2, 8, 128), jnp.int32),
            pltpu.VMEM((16, 1, 640), F32),
            pltpu.VMEM((1, 640), F32),
            pltpu.VMEM((1, 640), F32),
            pltpu.VMEM((128, 640), F32),
            pltpu.VMEM((80, 5120), BF),
            pltpu.VMEM((8, 80, 640), BF),
            pltpu.VMEM((640, 640), BF),
            pltpu.VMEM((2, 8, 48, 128), BF),
            pltpu.VMEM((32, 48, 128), BF),
            pltpu.VMEM((2, 48, 128), BF),
            pltpu.VMEM((8, 2, 48, 128), BF),
            pltpu.VMEM((8, 2, 64, 128), BF),
            pltpu.VMEM((8, 64, 128), BF),
            sem(7), sem(8), sem(8), sem(8), sem(8), sem(2), sem(2), sem(4), sem(4), sem(4), sem(4),
            sem(16), sem(32), sem(8), sem(8), sem(16), sem(8),
        ],
        compiler_params=pltpu.CompilerParams(
            collective_id=0, has_side_effects=True, vmem_limit_bytes=int(53.9 * 2**20)
        ),
        name="attend",
    )(
        queries.reshape(64, 5120),
        fresh_kv.reshape(2, 64, 1024),
        kv_pages.reshape(2, 128, 1024),
        page_list,
        tile_mask,
        out_weight,
    )
    return out.reshape(4, 16, 80)


def solution(mesh):
    return jax.shard_map(
        on_device,
        mesh=mesh,
        in_specs=(
            P("group", None, None),
            P(None, "group", None, None),
            P(None, ("group", "shard"), None, None),
            P("group", None),
            P("group", None),
            P("shard", None),
        ),
        out_specs=P("group", None, "shard"),
        check_vma=False,
    )
```

```python
import functools
import math

import jax
import jax.numpy as jnp
from jax import lax
from jax.experimental import pallas as pl
from jax.experimental.pallas import tpu as pltpu
from jax.sharding import PartitionSpec as P

MESH = pl.DeviceIdType.MESH
BF, F32 = jnp.bfloat16, jnp.float32
HIDDEN = -1e30
FLOOR = -1e29
FAR_FIRST = (12, 4, 11, 13, 3, 5, 10, 14, 2, 6, 9, 15, 1, 7, 8)


def device(h, m, y, z, c):
    return (h * 2 + c, (y * 8 + z) * 2 + (m + h) % 2)


def kernel(
    q_hbm, f_hbm, kv_hbm, list_hbm, mask_hbm, w_hbm, out_ref,
    list_ref, mask_ref, qb, qc, kvb, fb, eb, bias, m_ref, l_ref, acc, wv, wp, wb,
    msg, accr, attp, att_g, os, orv,
    loc, pg_s, pg_r, fw_s, fw_r, q_s, q_r, w_s, w_r, wx_s, wx_r,
    ac_s, ac_r, at_s, at_r, o_s, o_r,
):
    g = lax.axis_index("group")
    s = lax.axis_index("shard")
    h, c = g // 2, g % 2
    y, z, l = s // 16, (s // 2) % 8, s % 2
    m = (l + h) % 2
    head = 2 * y + m
    plane = [(0, 0), (1, 0), (0, 1), (0, 3), (1, 1), (1, 3), (0, 2), (1, 2)]
    column = [(dh, dz) for dh in range(2) for dz in range(8)]
    sibling = device(h, m, y, z, 1 - c)
    across = device(1 - h, m, y, z, c)

    def in_plane(j, core):
        dm, dy = plane[j]
        return device(h, (m + dm) % 2, (y + dy) % 4, z, core)

    def in_column(k, core):
        dh, dz = column[k]
        return device((h + dh) % 2, m, y, (z + dz) % 8, core)

    holder = z // 4 == m
    w_to = [2 * k + (z + c) % 2 for k in range(4)]

    def w_rows(zz, ll):
        return pl.ds(pl.multiple_of(80 * ((zz % 4) * 2 + ll), 16), 80)

    bar = pltpu.get_barrier_semaphore()

    def greet(d):
        pl.semaphore_signal(bar, inc=1, device_id=d, device_id_type=MESH)

    @pl.when(c == 1)
    def _():
        for k in FAR_FIRST:
            greet(in_column(k, 1))
            greet(in_column(k, 0))
        for j in range(7, 0, -1):
            greet(in_plane(j, 1))

    for j in range(7, 0, -1):
        greet(in_plane(j, 1 - c))
    greet(sibling)
    pl.when(c == 0)(lambda: greet(across))

    cols = pl.ds(pl.multiple_of(head * 128, 128), 128)
    q_cols = pl.ds(pl.multiple_of(head * 640, 128), 640)
    ld_q = pltpu.make_async_copy(q_hbm.at[:, q_cols], qb.at[0], loc.at[0])
    ld_kv = pltpu.make_async_copy(kv_hbm.at[:, :, cols], kvb.at[:, 0], loc.at[1])
    ld_f = pltpu.make_async_copy(f_hbm.at[:, :, cols], fb, loc.at[2])
    ld_w = pltpu.make_async_copy(w_hbm, wv, loc.at[3])
    ld_list = pltpu.make_async_copy(list_hbm, list_ref, loc.at[5])
    ld_mask = pltpu.make_async_copy(mask_hbm, mask_ref, loc.at[6])
    for ld in (ld_list, ld_mask, ld_q, ld_kv, ld_w, ld_f):
        ld.start()

    pl.semaphore_wait(bar, 24 + 6 * c)

    def send(src, dst, ss, rs, d):
        cp = pltpu.make_async_remote_copy(
            src_ref=src, dst_ref=dst, send_sem=ss, recv_sem=rs, device_id=d, device_id_type=MESH
        )
        cp.start()
        pending.append(cp)
        return cp

    def forward(j):
        return pltpu.make_async_remote_copy(
            src_ref=kvb.at[:, j], dst_ref=kvb.at[:, 8 + j], send_sem=fw_s.at[j], recv_sem=fw_r.at[j],
            device_id=sibling, device_id_type=MESH,
        )

    def pages_in(j):
        return pltpu.make_async_remote_copy(
            src_ref=kvb.at[:, 0], dst_ref=kvb.at[:, j], send_sem=pg_s.at[j], recv_sem=pg_r.at[j],
            device_id=sibling, device_id_type=MESH,
        )

    pending = []
    for j in range(1, 8):
        dm, dy = plane[j]
        there = 2 * ((y + dy) % 4) + (m + dm) % 2
        there_cols = pl.ds(pl.multiple_of(there * 128, 128), 128)
        send(kv_hbm.at[:, :, there_cols], kvb.at[:, j], pg_s.at[j], pg_r.at[j], in_plane(j, 1 - c))
    eb[0] = jnp.full((8, 128), -1, jnp.int32)
    ld_list.wait()
    ld_mask.wait()
    eb[0, 0:4, 0:64] = jnp.where(mask_ref[...] > 0, list_ref[...], -1)
    snd_e = send(eb.at[0], eb.at[1], q_s.at[0], q_r.at[0], across)
    ld_q.wait()
    snd_q = send(qb.at[0], qb.at[1], q_s.at[1], q_r.at[1], across)
    ld_kv.wait()

    forward(0).start()

    ld_w.wait()
    for z2 in range(8):
        wp[z2] = jnp.concatenate(
            [wv[:, 1280 * y2 + 160 * z2 : 1280 * y2 + 160 * z2 + 160] for y2 in range(4)], axis=1
        )

    def w_send(k):
        return pltpu.make_async_remote_copy(
            src_ref=wp.at[w_to[k]], dst_ref=wb.at[w_rows(z, l)], send_sem=w_s.at[k], recv_sem=w_r.at[z % 4],
            device_id=device(h, m, y, w_to[k], 1), device_id_type=MESH,
        )

    def w_cross(k):
        rows = wb.at[w_rows(k, l)]
        return pltpu.make_async_remote_copy(
            src_ref=rows, dst_ref=rows, send_sem=wx_s.at[k], recv_sem=wx_r.at[k], device_id=across, device_id_type=MESH
        )

    for k in range(4):
        pl.when(holder)(lambda: w_send(k).start())

    def w_pass_on(k):
        pltpu.make_async_remote_copy(
            src_ref=wp.at[0], dst_ref=wb.at[w_rows(k, l)], send_sem=w_s.at[k], recv_sem=w_r.at[k],
            device_id=across, device_id_type=MESH,
        ).wait_recv()
        w_cross(k).start()

    snd_e.wait_recv()
    lists = eb[...].reshape(16, 128)
    row = lax.broadcasted_iota(jnp.int32, (16, 640), 0)
    col = lax.broadcasted_iota(jnp.int32, (16, 640), 1)
    owner = jnp.where(col >= 320, 8, 0) + ((col >> 4) & 3)
    pick = (row == owner).astype(F32)
    for j in range(16):
        dm, dy = plane[j % 8]
        src_m, src_y, src_c = (m - dm + 2) % 2, (y - dy + 4) % 4, (c + j // 8 + min(j % 8, 1)) % 2
        src_l = (src_m + h) % 2
        number = (h * 2 + src_c) * 64 + (src_y * 8 + z) * 2 + src_l
        seen = jnp.max((lists == number).astype(F32), axis=1, keepdims=True)
        bias[j] = (jnp.sum(pick * seen, axis=0, keepdims=True) - 1.0) * (-HIDDEN)

    snd_q.wait_recv()
    for o in range(2):
        for i in range(5):
            qc[o * 320 + i * 64 : o * 320 + i * 64 + 64, :] = qb[o, :, i * 128 : i * 128 + 128]

    scale = math.log2(math.e) / math.sqrt(128)

    def scores(keys):
        return lax.dot_general(keys, qc[...], (((1,), (1,)), ((), ())), preferred_element_type=F32) * scale

    def weigh(values, weights):
        return lax.dot_general(
            values, weights.astype(BF), (((0,), (0,)), ((), ())), preferred_element_type=F32
        )

    ld_f.wait()
    key = lax.broadcasted_iota(jnp.int32, (64, 640), 0)
    col = lax.broadcasted_iota(jnp.int32, (64, 640), 1)
    visible = (col < 320) & ((key >> 4) == ((col >> 4) & 3)) & ((key & 15) <= (col & 15)) & (z == 0)
    sc = jnp.where(visible, scores(fb[0]), HIDDEN)
    top = jnp.maximum(jnp.max(sc, axis=0, keepdims=True), FLOOR)
    wt = jnp.exp2(sc - top)
    m_ref[...] = top
    l_ref[...] = jnp.sum(wt, axis=0, keepdims=True)
    acc[...] = weigh(fb[1], wt)

    @pl.loop(0, 8)
    def _(n):
        phase, pair = n // 2, n % 2

        @pl.when(phase % 2 == 0)
        def _():
            for j in range(2):
                slot = 2 * phase + 2 * pair + j

                @pl.when(slot > 0)
                def _():
                    pages_in(slot).wait_recv()
                    forward(slot).start()

        @pl.when(phase % 2 == 1)
        def _():
            for j in range(2):
                forward(2 * (phase - 1) + 2 * pair + j).wait_recv()

        slots = pl.ds((phase % 2) * 8 + (phase // 2) * 4 + 2 * pair, 2)
        sc = scores(kvb[0, slots].reshape(256, 128))
        sc = (sc.reshape(2, 128, 640) + bias[slots]).reshape(256, 640)
        old = m_ref[...]
        top = jnp.maximum(old, jnp.max(sc, axis=0, keepdims=True))
        keep = jnp.exp2(old - top)
        wt = jnp.exp2(sc - top)
        m_ref[...] = top
        l_ref[...] = l_ref[...] * keep + jnp.sum(wt, axis=0, keepdims=True)
        acc[...] = acc[...] * keep + weigh(kvb[1, slots].reshape(256, 128), wt)

    def pieces(x, n):
        out = []
        for _ in range(n):
            out.append(x.astype(BF).astype(F32))
            x = x - out[-1]
        return out

    sums_rows = acc[...].T
    stats = jnp.concatenate(
        pieces(m_ref[...], 3) + pieces(l_ref[...], 2) + [jnp.zeros((3, 640), F32)], axis=0
    )
    def fill(o):
        for k in range(8):
            at = slice(o * 320 + k * 40, o * 320 + k * 40 + 40)
            tail = jnp.concatenate([stats[:, at], jnp.zeros((8, 88), F32)], axis=1)
            msg[o, k] = jnp.concatenate([sums_rows[at], tail], axis=0).astype(BF)

    def part(half, dz):
        dh = (half + h) % 2
        k = dh * 8 + dz
        return pltpu.make_async_remote_copy(
            src_ref=msg.at[dh, (z + dz) % 8], dst_ref=accr.at[c * 16 + k], send_sem=ac_s.at[k], recv_sem=ac_r.at[c * 16 + k],
            device_id=device(half, m, y, (z + dz) % 8, 1), device_id_type=MESH,
        )

    def part_in(i):
        return pltpu.make_async_remote_copy(
            src_ref=msg.at[0, 0], dst_ref=accr.at[i], send_sem=ac_s.at[0], recv_sem=ac_r.at[i],
            device_id=sibling, device_id_type=MESH,
        )

    def piece_to(dz):
        return pltpu.make_async_remote_copy(
            src_ref=attp, dst_ref=att_g.at[z], send_sem=at_s.at[dz], recv_sem=at_r.at[dz],
            device_id=in_column(dz, 1), device_id_type=MESH,
        )

    def out_to(j, core):
        dm, dy = plane[j]
        k = 2 * ((y + dy) % 4) + ((m + dm) % 2 + h) % 2
        return pltpu.make_async_remote_copy(
            src_ref=os.at[k, core], dst_ref=orv.at[j], send_sem=o_s.at[core * 8 + j], recv_sem=o_r.at[j],
            device_id=in_plane(j, core), device_id_type=MESH,
        )

    fill(0)
    fill(1)
    others = [(half, dz) for dz in (4, 3, 5, 2, 6, 1, 7) for half in range(2)] + [(1 - h, 0)]
    for half, dz in others:
        part(half, dz).start()
    pl.when(c == 0)(lambda: part(h, 0).start())

    @pl.when(c == 1)
    def _():
        accr[16] = msg[0, z]
        for k in range(4):
            w_pass_on(k)
        for i in range(32):
            if i != 16:
                part_in(i).wait_recv()
        stats = accr[:, 32:48, :].astype(F32)
        tops = (stats[:, 8] + stats[:, 9] + stats[:, 10]).reshape(2, 16, 128)
        sums = (stats[:, 11] + stats[:, 12]).reshape(2, 16, 128)
        factor = jnp.exp2(tops - jnp.max(tops, axis=1, keepdims=True))
        factor = (factor / jnp.sum(factor * sums, axis=1, keepdims=True)).reshape(32, 128).T
        for i in range(2):
            total = jnp.zeros((40, 128), F32)
            for k in range(16 * i, 16 * i + 16):
                total = total + accr[k].astype(F32)[0:40] * factor[0:40, k : k + 1]
            attp[i] = jnp.concatenate([total, jnp.zeros((8, 128), F32)], axis=0).astype(BF)
        for dz in (4, 3, 5, 2, 6, 1, 7):
            piece_to(dz).start()
        att_g[z] = attp[...]
        for k in range(4):
            pltpu.make_async_remote_copy(
                src_ref=wp.at[0], dst_ref=wb.at[w_rows(k, 1 - l)], send_sem=wx_s.at[k], recv_sem=wx_r.at[k],
                device_id=across, device_id_type=MESH,
            ).wait_recv()
        for dz in range(1, 8):
            pltpu.make_async_remote_copy(
                src_ref=attp, dst_ref=att_g.at[(z - dz + 8) % 8], send_sem=at_s.at[dz], recv_sem=at_r.at[dz],
                device_id=sibling, device_id_type=MESH,
            ).wait_recv()
        att = [att_g[:, i].astype(F32)[:, :40].reshape(320, 128).astype(BF) for i in range(2)]
        proj = jnp.zeros((128, 640), F32)
        for i in range(5):
            rows = slice(i * 64, i * 64 + 64)
            proj += jnp.dot(
                jnp.concatenate([att[0][rows], att[1][rows]], axis=0), wb[i * 128 : i * 128 + 128, :],
                preferred_element_type=F32,
            )
        proj = proj.astype(BF)
        for k in range(8):
            for i in range(2):
                os[k, i, :, 0:80] = proj[64 * i : 64 * i + 64, 80 * k : 80 * k + 80]
        for j in range(7, -1, -1):
            out_to(j, 0).start()
            if j:
                out_to(j, 1).start()
        orv[0] = os[2 * y + l, 1]

    result = jnp.zeros((64, 128), F32)
    pl.when(c == 0)(lambda: out_to(0, 0).wait_recv())
    for j in range(7, -1, -1):
        if j:
            out_to(j, 0).wait_recv()
        result += orv[j].astype(F32)
    out_ref[...] = result[:, :80].astype(BF)

    for cp in pending:
        cp.wait_send()
    for j in range(8):
        forward(j).wait_send()
    for k in range(4):
        pl.when(holder)(lambda: w_send(k).wait_send())
    for half, dz in others:
        part(half, dz).wait_send()
    pl.when(c == 0)(lambda: part(h, 0).wait_send())

    @pl.when(c == 1)
    def _():
        for k in range(4):
            w_cross(k).wait_send()
        for dz in range(1, 8):
            piece_to(dz).wait_send()
        for j in range(8):
            out_to(j, 0).wait_send()
            if j:
                out_to(j, 1).wait_send()


def on_device(queries, fresh_kv, kv_pages, page_list, tile_mask, out_weight):
    hbm, vmem = pl.BlockSpec(memory_space=pltpu.HBM), pl.BlockSpec(memory_space=pltpu.VMEM)
    sem = lambda n: pltpu.SemaphoreType.DMA((n,))
    out = pl.pallas_call(
        kernel,
        out_shape=jax.ShapeDtypeStruct((64, 80), BF),
        in_specs=[hbm] * 6,
        out_specs=vmem,
        scratch_shapes=[
            pltpu.VMEM((4, 64), jnp.int32),
            pltpu.VMEM((4, 64), jnp.int32),
            pltpu.VMEM((2, 64, 640), BF),
            pltpu.VMEM((640, 128), BF),
            pltpu.VMEM((2, 16, 128, 128), BF),
            pltpu.VMEM((2, 64, 128), BF),
            pltpu.VMEM((2, 8, 128), jnp.int32),
            pltpu.VMEM((16, 1, 640), F32),
            pltpu.VMEM((1, 640), F32),
            pltpu.VMEM((1, 640), F32),
            pltpu.VMEM((128, 640), F32),
            pltpu.VMEM((80, 5120), BF),
            pltpu.VMEM((8, 80, 640), BF),
            pltpu.VMEM((640, 640), BF),
            pltpu.VMEM((2, 8, 48, 128), BF),
            pltpu.VMEM((32, 48, 128), BF),
            pltpu.VMEM((2, 48, 128), BF),
            pltpu.VMEM((8, 2, 48, 128), BF),
            pltpu.VMEM((8, 2, 64, 128), BF),
            pltpu.VMEM((8, 64, 128), BF),
            sem(7), sem(8), sem(8), sem(8), sem(8), sem(2), sem(2), sem(4), sem(4), sem(4), sem(4),
            sem(16), sem(32), sem(8), sem(8), sem(16), sem(8),
        ],
        compiler_params=pltpu.CompilerParams(
            collective_id=0, has_side_effects=True, vmem_limit_bytes=int(53.9 * 2**20)
        ),
        name="attend",
    )(
        queries.reshape(64, 5120),
        fresh_kv.reshape(2, 64, 1024),
        kv_pages.reshape(2, 128, 1024),
        page_list,
        tile_mask,
        out_weight,
    )
    return out.reshape(4, 16, 80)


def solution(mesh):
    return jax.shard_map(
        on_device,
        mesh=mesh,
        in_specs=(
            P("group", None, None),
            P(None, "group", None, None),
            P(None, ("group", "shard"), None, None),
            P("group", None),
            P("group", None),
            P("shard", None),
        ),
        out_specs=P("group", None, "shard"),
        check_vma=False,
    )
```

```python
import functools
import math

import jax
import jax.numpy as jnp
from jax import lax
from jax.experimental import pallas as pl
from jax.experimental.pallas import tpu as pltpu
from jax.sharding import PartitionSpec as P

MESH = pl.DeviceIdType.MESH
BF, F32 = jnp.bfloat16, jnp.float32
HIDDEN = -1e30
FLOOR = -1e29
FAR_FIRST = (12, 4, 11, 13, 3, 5, 10, 14, 2, 6, 9, 15, 1, 7, 8)


def device(h, m, y, z, c):
    return (h * 2 + c, (y * 8 + z) * 2 + (m + h) % 2)


def kernel(
    q_hbm, f_hbm, kv_hbm, list_hbm, mask_hbm, w_hbm, out_ref,
    list_ref, mask_ref, qb, qc, kvb, fb, eb, bias, m_ref, l_ref, acc, wv, wp, wb,
    msg, accr, attp, att_g, os, orv,
    loc, pg_s, pg_r, fw_s, fw_r, q_s, q_r, w_s, w_r, wx_s, wx_r,
    ac_s, ac_r, at_s, at_r, o_s, o_r,
):
    g = lax.axis_index("group")
    s = lax.axis_index("shard")
    h, c = g // 2, g % 2
    y, z, l = s // 16, (s // 2) % 8, s % 2
    m = (l + h) % 2
    head = 2 * y + m
    plane = [(0, 0), (1, 0), (0, 1), (0, 3), (1, 1), (1, 3), (0, 2), (1, 2)]
    column = [(dh, dz) for dh in range(2) for dz in range(8)]
    sibling = device(h, m, y, z, 1 - c)
    across = device(1 - h, m, y, z, c)

    def in_plane(j, core):
        dm, dy = plane[j]
        return device(h, (m + dm) % 2, (y + dy) % 4, z, core)

    def in_column(k, core):
        dh, dz = column[k]
        return device((h + dh) % 2, m, y, (z + dz) % 8, core)

    holder = z // 4 == m
    w_to = [2 * k + (z + c) % 2 for k in range(4)]

    def w_rows(zz, ll):
        return pl.ds(pl.multiple_of(80 * ((zz % 4) * 2 + ll), 16), 80)

    bar = pltpu.get_barrier_semaphore()

    def greet(d):
        pl.semaphore_signal(bar, inc=1, device_id=d, device_id_type=MESH)

    @pl.when(c == 1)
    def _():
        for k in FAR_FIRST:
            greet(in_column(k, 1))
            greet(in_column(k, 0))
        for j in range(7, 0, -1):
            greet(in_plane(j, 1))

    for j in range(7, 0, -1):
        greet(in_plane(j, 1 - c))
    greet(sibling)
    pl.when(c == 0)(lambda: greet(across))

    cols = pl.ds(pl.multiple_of(head * 128, 128), 128)
    q_cols = pl.ds(pl.multiple_of(head * 640, 128), 640)
    ld_q = pltpu.make_async_copy(q_hbm.at[:, q_cols], qb.at[0], loc.at[0])
    ld_kv = pltpu.make_async_copy(kv_hbm.at[:, :, cols], kvb.at[:, 0], loc.at[1])
    ld_f = pltpu.make_async_copy(f_hbm.at[:, :, cols], fb, loc.at[2])
    ld_w = pltpu.make_async_copy(w_hbm, wv, loc.at[3])
    ld_list = pltpu.make_async_copy(list_hbm, list_ref, loc.at[5])
    ld_mask = pltpu.make_async_copy(mask_hbm, mask_ref, loc.at[6])
    for ld in (ld_list, ld_mask, ld_q, ld_kv, ld_w, ld_f):
        ld.start()

    pl.semaphore_wait(bar, 24 + 6 * c)

    def send(src, dst, ss, rs, d):
        cp = pltpu.make_async_remote_copy(
            src_ref=src, dst_ref=dst, send_sem=ss, recv_sem=rs, device_id=d, device_id_type=MESH
        )
        cp.start()
        pending.append(cp)
        return cp

    def forward(j):
        return pltpu.make_async_remote_copy(
            src_ref=kvb.at[:, j], dst_ref=kvb.at[:, 8 + j], send_sem=fw_s.at[j], recv_sem=fw_r.at[j],
            device_id=sibling, device_id_type=MESH,
        )

    def pages_in(j):
        return pltpu.make_async_remote_copy(
            src_ref=kvb.at[:, 0], dst_ref=kvb.at[:, j], send_sem=pg_s.at[j], recv_sem=pg_r.at[j],
            device_id=sibling, device_id_type=MESH,
        )

    pending = []
    for j in range(1, 8):
        dm, dy = plane[j]
        there = 2 * ((y + dy) % 4) + (m + dm) % 2
        there_cols = pl.ds(pl.multiple_of(there * 128, 128), 128)
        send(kv_hbm.at[:, :, there_cols], kvb.at[:, j], pg_s.at[j], pg_r.at[j], in_plane(j, 1 - c))
    eb[0] = jnp.full((8, 128), -1, jnp.int32)
    ld_list.wait()
    ld_mask.wait()
    eb[0, 0:4, 0:64] = jnp.where(mask_ref[...] > 0, list_ref[...], -1)
    snd_e = send(eb.at[0], eb.at[1], q_s.at[0], q_r.at[0], across)
    ld_q.wait()
    snd_q = send(qb.at[0], qb.at[1], q_s.at[1], q_r.at[1], across)
    ld_kv.wait()

    forward(0).start()

    ld_w.wait()
    for z2 in range(8):
        wp[z2] = jnp.concatenate(
            [wv[:, 1280 * y2 + 160 * z2 : 1280 * y2 + 160 * z2 + 160] for y2 in range(4)], axis=1
        )

    def w_send(k):
        return pltpu.make_async_remote_copy(
            src_ref=wp.at[w_to[k]], dst_ref=wb.at[w_rows(z, l)], send_sem=w_s.at[k], recv_sem=w_r.at[z % 4],
            device_id=device(h, m, y, w_to[k], 1), device_id_type=MESH,
        )

    def w_cross(k):
        rows = wb.at[w_rows(k, l)]
        return pltpu.make_async_remote_copy(
            src_ref=rows, dst_ref=rows, send_sem=wx_s.at[k], recv_sem=wx_r.at[k], device_id=across, device_id_type=MESH
        )

    for k in range(4):
        pl.when(holder)(lambda: w_send(k).start())

    def w_pass_on(k):
        pltpu.make_async_remote_copy(
            src_ref=wp.at[0], dst_ref=wb.at[w_rows(k, l)], send_sem=w_s.at[k], recv_sem=w_r.at[k],
            device_id=across, device_id_type=MESH,
        ).wait_recv()
        w_cross(k).start()

    snd_e.wait_recv()
    lists = eb[...].reshape(16, 128)
    row = lax.broadcasted_iota(jnp.int32, (16, 640), 0)
    col = lax.broadcasted_iota(jnp.int32, (16, 640), 1)
    owner = jnp.where(col >= 320, 8, 0) + ((col >> 4) & 3)
    pick = (row == owner).astype(F32)
    for j in range(16):
        dm, dy = plane[j % 8]
        src_m, src_y, src_c = (m - dm + 2) % 2, (y - dy + 4) % 4, (c + j // 8 + min(j % 8, 1)) % 2
        src_l = (src_m + h) % 2
        number = (h * 2 + src_c) * 64 + (src_y * 8 + z) * 2 + src_l
        seen = jnp.max((lists == number).astype(F32), axis=1, keepdims=True)
        bias[j] = (jnp.sum(pick * seen, axis=0, keepdims=True) - 1.0) * (-HIDDEN)

    snd_q.wait_recv()
    for o in range(2):
        for i in range(5):
            qc[o * 320 + i * 64 : o * 320 + i * 64 + 64, :] = qb[o, :, i * 128 : i * 128 + 128]

    scale = math.log2(math.e) / math.sqrt(128)

    def scores(keys):
        return lax.dot_general(keys, qc[...], (((1,), (1,)), ((), ())), preferred_element_type=F32) * scale

    def weigh(values, weights):
        return lax.dot_general(
            values, weights.astype(BF), (((0,), (0,)), ((), ())), preferred_element_type=F32
        )

    ld_f.wait()
    key = lax.broadcasted_iota(jnp.int32, (64, 640), 0)
    col = lax.broadcasted_iota(jnp.int32, (64, 640), 1)
    visible = (col < 320) & ((key >> 4) == ((col >> 4) & 3)) & ((key & 15) <= (col & 15)) & (z == 0)
    sc = jnp.where(visible, scores(fb[0]), HIDDEN)
    top = jnp.maximum(jnp.max(sc, axis=0, keepdims=True), FLOOR)
    wt = jnp.exp2(sc - top)
    m_ref[...] = top
    l_ref[...] = jnp.sum(wt, axis=0, keepdims=True)
    acc[...] = weigh(fb[1], wt)

    @pl.loop(0, 8)
    def _(n):
        phase, pair = n // 2, n % 2

        @pl.when(phase % 2 == 0)
        def _():
            for j in range(2):
                slot = 2 * phase + 2 * pair + j

                @pl.when(slot > 0)
                def _():
                    pages_in(slot).wait_recv()
                    forward(slot).start()

        @pl.when(phase % 2 == 1)
        def _():
            for j in range(2):
                forward(2 * (phase - 1) + 2 * pair + j).wait_recv()

        slots = pl.ds((phase % 2) * 8 + (phase // 2) * 4 + 2 * pair, 2)
        sc = scores(kvb[0, slots].reshape(256, 128))
        sc = (sc.reshape(2, 128, 640) + bias[slots]).reshape(256, 640)
        old = m_ref[...]
        top = jnp.maximum(old, jnp.max(sc, axis=0, keepdims=True))
        keep = jnp.exp2(old - top)
        wt = jnp.exp2(sc - top)
        m_ref[...] = top
        l_ref[...] = l_ref[...] * keep + jnp.sum(wt, axis=0, keepdims=True)
        acc[...] = acc[...] * keep + weigh(kvb[1, slots].reshape(256, 128), wt)

    def pieces(x, n):
        out = []
        for _ in range(n):
            out.append(x.astype(BF).astype(F32))
            x = x - out[-1]
        return out

    sums_rows = acc[...].T
    stats = jnp.concatenate(
        pieces(m_ref[...], 3) + pieces(l_ref[...], 2) + [jnp.zeros((3, 640), F32)], axis=0
    )
    def fill(o):
        for k in range(8):
            at = slice(o * 320 + k * 40, o * 320 + k * 40 + 40)
            tail = jnp.concatenate([stats[:, at], jnp.zeros((8, 88), F32)], axis=1)
            msg[o, k] = jnp.concatenate([sums_rows[at], tail], axis=0).astype(BF)

    def part(half, dz):
        dh = (half + h) % 2
        k = dh * 8 + dz
        return pltpu.make_async_remote_copy(
            src_ref=msg.at[dh, (z + dz) % 8], dst_ref=accr.at[c * 16 + k], send_sem=ac_s.at[k], recv_sem=ac_r.at[c * 16 + k],
            device_id=device(half, m, y, (z + dz) % 8, 1), device_id_type=MESH,
        )

    def part_in(i):
        return pltpu.make_async_remote_copy(
            src_ref=msg.at[0, 0], dst_ref=accr.at[i], send_sem=ac_s.at[0], recv_sem=ac_r.at[i],
            device_id=sibling, device_id_type=MESH,
        )

    def piece_to(dz):
        return pltpu.make_async_remote_copy(
            src_ref=attp, dst_ref=att_g.at[z], send_sem=at_s.at[dz], recv_sem=at_r.at[dz],
            device_id=in_column(dz, 1), device_id_type=MESH,
        )

    def out_to(j, core):
        dm, dy = plane[j]
        k = 2 * ((y + dy) % 4) + ((m + dm) % 2 + h) % 2
        return pltpu.make_async_remote_copy(
            src_ref=os.at[k, core], dst_ref=orv.at[j], send_sem=o_s.at[core * 8 + j], recv_sem=o_r.at[j],
            device_id=in_plane(j, core), device_id_type=MESH,
        )

    fill(0)
    fill(1)
    others = [(half, dz) for dz in (4, 3, 5, 2, 6, 1, 7) for half in range(2)] + [(1 - h, 0)]
    for half, dz in others:
        part(half, dz).start()
    pl.when(c == 0)(lambda: part(h, 0).start())

    @pl.when(c == 1)
    def _():
        accr[16] = msg[0, z]
        for k in range(4):
            w_pass_on(k)
        for i in range(32):
            if i != 16:
                part_in(i).wait_recv()
        stats = accr[:, 32:48, :].astype(F32)
        tops = (stats[:, 8] + stats[:, 9] + stats[:, 10]).reshape(2, 16, 128)
        sums = (stats[:, 11] + stats[:, 12]).reshape(2, 16, 128)
        factor = jnp.exp2(tops - jnp.max(tops, axis=1, keepdims=True))
        factor = (factor / jnp.sum(factor * sums, axis=1, keepdims=True)).reshape(32, 128).T
        for i in range(2):
            total = jnp.zeros((40, 128), F32)
            for k in range(16 * i, 16 * i + 16):
                total = total + accr[k].astype(F32)[0:40] * factor[0:40, k : k + 1]
            attp[i] = jnp.concatenate([total, jnp.zeros((8, 128), F32)], axis=0).astype(BF)
        for dz in (4, 3, 5, 2, 6, 1, 7):
            piece_to(dz).start()
        att_g[z] = attp[...]
        for k in range(4):
            pltpu.make_async_remote_copy(
                src_ref=wp.at[0], dst_ref=wb.at[w_rows(k, 1 - l)], send_sem=wx_s.at[k], recv_sem=wx_r.at[k],
                device_id=across, device_id_type=MESH,
            ).wait_recv()
        for dz in range(1, 8):
            pltpu.make_async_remote_copy(
                src_ref=attp, dst_ref=att_g.at[(z - dz + 8) % 8], send_sem=at_s.at[dz], recv_sem=at_r.at[dz],
                device_id=sibling, device_id_type=MESH,
            ).wait_recv()
        att = [att_g[:, i].astype(F32)[:, :40].reshape(320, 128).astype(BF) for i in range(2)]
        proj = jnp.zeros((128, 640), F32)
        for i in range(5):
            rows = slice(i * 64, i * 64 + 64)
            proj += jnp.dot(
                jnp.concatenate([att[0][rows], att[1][rows]], axis=0), wb[i * 128 : i * 128 + 128, :],
                preferred_element_type=F32,
            )
        proj = proj.astype(BF)
        for k in range(8):
            for i in range(2):
                os[k, i, :, 0:80] = proj[64 * i : 64 * i + 64, 80 * k : 80 * k + 80]
        for j in range(7, -1, -1):
            if j:
                out_to(j, 1).start()
            out_to(j, 0).start()
        orv[0] = os[2 * y + l, 1]

    result = jnp.zeros((64, 128), F32)
    pl.when(c == 0)(lambda: out_to(0, 0).wait_recv())
    for j in range(7, -1, -1):
        if j:
            out_to(j, 0).wait_recv()
        result += orv[j].astype(F32)
    out_ref[...] = result[:, :80].astype(BF)

    for cp in pending:
        cp.wait_send()
    for j in range(8):
        forward(j).wait_send()
    for k in range(4):
        pl.when(holder)(lambda: w_send(k).wait_send())
    for half, dz in others:
        part(half, dz).wait_send()
    pl.when(c == 0)(lambda: part(h, 0).wait_send())

    @pl.when(c == 1)
    def _():
        for k in range(4):
            w_cross(k).wait_send()
        for dz in range(1, 8):
            piece_to(dz).wait_send()
        for j in range(8):
            out_to(j, 0).wait_send()
            if j:
                out_to(j, 1).wait_send()


def on_device(queries, fresh_kv, kv_pages, page_list, tile_mask, out_weight):
    hbm, vmem = pl.BlockSpec(memory_space=pltpu.HBM), pl.BlockSpec(memory_space=pltpu.VMEM)
    sem = lambda n: pltpu.SemaphoreType.DMA((n,))
    out = pl.pallas_call(
        kernel,
        out_shape=jax.ShapeDtypeStruct((64, 80), BF),
        in_specs=[hbm] * 6,
        out_specs=vmem,
        scratch_shapes=[
            pltpu.VMEM((4, 64), jnp.int32),
            pltpu.VMEM((4, 64), jnp.int32),
            pltpu.VMEM((2, 64, 640), BF),
            pltpu.VMEM((640, 128), BF),
            pltpu.VMEM((2, 16, 128, 128), BF),
            pltpu.VMEM((2, 64, 128), BF),
            pltpu.VMEM((2, 8, 128), jnp.int32),
            pltpu.VMEM((16, 1, 640), F32),
            pltpu.VMEM((1, 640), F32),
            pltpu.VMEM((1, 640), F32),
            pltpu.VMEM((128, 640), F32),
            pltpu.VMEM((80, 5120), BF),
            pltpu.VMEM((8, 80, 640), BF),
            pltpu.VMEM((640, 640), BF),
            pltpu.VMEM((2, 8, 48, 128), BF),
            pltpu.VMEM((32, 48, 128), BF),
            pltpu.VMEM((2, 48, 128), BF),
            pltpu.VMEM((8, 2, 48, 128), BF),
            pltpu.VMEM((8, 2, 64, 128), BF),
            pltpu.VMEM((8, 64, 128), BF),
            sem(7), sem(8), sem(8), sem(8), sem(8), sem(2), sem(2), sem(4), sem(4), sem(4), sem(4),
            sem(16), sem(32), sem(8), sem(8), sem(16), sem(8),
        ],
        compiler_params=pltpu.CompilerParams(
            collective_id=0, has_side_effects=True, vmem_limit_bytes=int(53.9 * 2**20)
        ),
        name="attend",
    )(
        queries.reshape(64, 5120),
        fresh_kv.reshape(2, 64, 1024),
        kv_pages.reshape(2, 128, 1024),
        page_list,
        tile_mask,
        out_weight,
    )
    return out.reshape(4, 16, 80)


def solution(mesh):
    return jax.shard_map(
        on_device,
        mesh=mesh,
        in_specs=(
            P("group", None, None),
            P(None, "group", None, None),
            P(None, ("group", "shard"), None, None),
            P("group", None),
            P("group", None),
            P("shard", None),
        ),
        out_specs=P("group", None, "shard"),
        check_vma=False,
    )
```
